512 devices in a mesh: seq: 32 (over z, core), head: 16 (over y, x).
Axes of the slice: x: 4, y: 4, z: 16, core: 2. Of those that a mesh axis runs over, the one named last changes fastest.
Arguments:
- light_query: bfloat16 [8192, 8192], P('seq', 'head'), may hold values from -6 to 6
- light_keys: bfloat16 [8192, 8192], P('seq', 'head'), may hold values from -6 to 6
- light_values: bfloat16 [8192, 8192], P('seq', 'head'), may hold values from -6 to 6
- log_decay: float32 [64, 8192], P('head', 'seq'), may hold values from -1.45 to 0, as said below
- light_gain: float32 [8192], P('head'), may hold values from 0.25 to 1.75
- query2: bfloat16 [8192, 8192], P('seq', 'head'), may hold values from -80 to 80
- keys2: bfloat16 [8192, 1024], P('seq'), may hold values from -4 to 4
- values2: bfloat16 [8192, 1024], P('seq'), may hold values from -6 to 6
Outputs:
- light_out: bfloat16 [8192, 8192], P('seq', 'head')
- soft_out: bfloat16 [8192, 8192], P('seq', 'head')
The draws below stay inside these ranges and needn't reach their ends.
Inputs may be any that keep to these rules, and one draw needn't show every extreme that they name: `log_decay`: strictly negative.
All inputs are finite; a program needn't handle non-finite values.
Results may differ from the reference program's by a relative error of at most 0.0095.
Values may be sent and summed in bfloat16 or wider, within the bound.
No kernel may reach another device: no remote copies, remote signals or barrier semaphores. Data moves between devices by JAX's collectives and lax.ppermute only.
A program may use at most 64 MiB of HBM per device.

```python
import math
import jax
import jax.numpy as jnp
from jax import lax

HEADS = 64
HD = 128
KVH = 8
BLOCK = 256
TOKENS = 8192


def key_table(key):
    base = jnp.clip(jax.random.normal(key, (TOKENS, KVH * HD), jnp.float32), -4.0, 4.0)
    for index in range(6):
        head_number = index * 21 % HEADS
        kv_head = head_number // (HEADS // KVH)
        row_number = 2 * index
        left = kv_head * HD
        mixed_row = base[row_number + 1, left:left + HD]
        base = base.at[row_number + 1, left:left + HD].set(mixed_row)
    return base


def draw_keys2(key, part):
    table = key_table(key)
    return table.astype(jnp.bfloat16)


def draw_query2(key, part):
    own_key = jax.random.fold_in(key, 11)
    queries = jnp.clip(jax.random.normal(own_key, (TOKENS, HEADS * HD), jnp.float32), -6.0, 6.0)
    return queries.astype(jnp.bfloat16)


def draw_log_decay(key, part):
    key = jax.random.fold_in(key, 3)
    subkeys = jax.random.split(key, 6)
    fast_share = 0.5
    picked = jax.random.uniform(subkeys[0], (HEADS,), jnp.float32) < fast_share
    slow_rate = jax.random.uniform(subkeys[1], (HEADS,), jnp.float32, 0.1, 0.3) * math.log(10.0) / TOKENS
    fast_rate = jax.random.uniform(subkeys[2], (HEADS,), jnp.float32, 1.0 / 50.0, 1.0 / 30.0)
    decay_speed = jnp.where(picked, fast_rate, slow_rate)
    coarse_scores = jax.random.uniform(subkeys[3], (HEADS, TOKENS), jnp.float32, 0.5, 1.5)
    token_locations = jax.random.randint(subkeys[4], (2,), 0, TOKENS)
    layer_depth = jax.random.uniform(subkeys[5], (2,), jnp.float32, 0.22, 0.69)
    device_slots = jnp.arange(TOKENS)
    attention_spike = jnp.sum(layer_depth[:, None] * (device_slots[None, :] == token_locations[:, None]).astype(jnp.float32), axis=0)
    return -decay_speed[:, None] * coarse_scores - attention_spike[None, :]


def shard_levels(key, dims, cuts, smallest, top_value):
    gain, own = 1.0, jax.random.fold_in(key, 6)
    for position, blocks in cuts:
        draws = jnp.exp(jax.random.uniform(jax.random.fold_in(own, position), (blocks,), jnp.float32, smallest / len(cuts), top_value / len(cuts)))
        gain = gain * jnp.repeat(draws, dims[position] // blocks).reshape([-1 if axis == position else 1 for axis in range(len(dims))])
    return gain


def noise(key, shape, width, most, cuts=(), held_as=jnp.bfloat16):
    values = jax.random.normal(key, shape, jnp.float32) * width
    if len(cuts) > 0:
        values = shard_levels(key, shape, cuts, -0.22, 0.18) * values
    return jnp.clip(values, min=-most, max=most).astype(held_as)


def setup_inputs(seed: int = 0) -> dict:
    seeds = jax.random.split(jax.random.key(seed), 9)
    light_query = noise(seeds[0], (TOKENS, HEADS * HD), 1.0, 6.0, ((0, 32), (1, 16)))
    light_keys = noise(seeds[1], (TOKENS, HEADS * HD), 1.0, 6.0, ((0, 32), (1, 16)))
    light_values = noise(seeds[2], (TOKENS, HEADS * HD), 1.0, 6.0, ((0, 32), (1, 16)))
    log_decay = draw_log_decay(jax.random.fold_in(seeds[8], 71), 0)
    light_gain = jnp.clip(1.0 + 0.15 * jax.random.normal(seeds[4], (HEADS * HD,), jnp.float32), 0.25, 1.75)
    query2 = draw_query2(jax.random.fold_in(seeds[8], 71), 0)
    keys2 = draw_keys2(jax.random.fold_in(seeds[8], 71), 0)
    values2 = noise(seeds[7], (TOKENS, KVH * HD), 1.0, 6.0, ((0, 32),))
    return dict(light_query=light_query, light_keys=light_keys, light_values=light_values, log_decay=log_decay, light_gain=light_gain, query2=query2, keys2=keys2, values2=values2)


def lightning(light_query, light_keys, light_values, log_decay, light_gain):
    nblocks = TOKENS // BLOCK
    queries = light_query.reshape(nblocks, BLOCK, HEADS, HD)
    keys_all = light_keys.reshape(nblocks, BLOCK, HEADS, HD)
    values_all = light_values.reshape(nblocks, BLOCK, HEADS, HD)
    decays = log_decay.reshape(HEADS, nblocks, BLOCK).transpose(1, 0, 2)
    lower = jnp.tril(jnp.ones((BLOCK, BLOCK), dtype=bool))
    highest = lax.Precision.HIGHEST

    def advance(state, item):
        query_blk, key_blk, value_blk, decay_blk = item
        running = jnp.cumsum(decay_blk, axis=1)
        scores = jnp.einsum('ihd,jhd->hij', query_blk.astype(jnp.float32), key_blk.astype(jnp.float32), precision=highest)
        spread = jnp.where(lower, running[:, :, None] - running[:, None, :], 0.0)
        weighted = jnp.where(lower, scores * jnp.exp(spread), 0.0)
        weighted = lax.optimization_barrier(weighted.astype(jnp.bfloat16)).astype(jnp.float32)
        within = jnp.einsum('hij,jhd->ihd', weighted, value_blk.astype(jnp.float32), precision=highest)
        tail = jnp.exp(running[:, -1:] - running)
        scaled_keys = key_blk.astype(jnp.float32) * tail.T[:, :, None]
        scaled_keys = lax.optimization_barrier(scaled_keys.astype(jnp.bfloat16)).astype(jnp.float32)
        block_state = jnp.einsum('jhd,jhe->hde', scaled_keys, value_blk.astype(jnp.float32), precision=highest)
        lifted = query_blk.astype(jnp.float32) * jnp.exp(running).T[:, :, None]
        across = jnp.einsum('ihd,hde->ihe', lifted, state, precision=highest)
        new_state = jnp.exp(running[:, -1])[:, None, None] * state + block_state
        return (new_state, within + across)
    start = jnp.zeros((HEADS, HD, HD), jnp.float32)
    _, mixed = lax.scan(advance, start, (queries, keys_all, values_all, decays))
    normed = mixed * lax.rsqrt(lax.optimization_barrier(jnp.mean(mixed * mixed, axis=-1, keepdims=True)) + 1e-06)
    return (normed.reshape(TOKENS, HEADS * HD) * light_gain).astype(jnp.bfloat16)

def softmax_attention_layer(query2, keys2, values2):
    group = HEADS // KVH
    query_heads = query2.reshape(TOKENS, KVH, group, HD).transpose(1, 0, 2, 3)
    key_heads = keys2.reshape(TOKENS, KVH, HD).transpose(1, 0, 2)
    value_heads = values2.reshape(TOKENS, KVH, HD).transpose(1, 0, 2)
    rows_blk = min(512, TOKENS)
    nquery = TOKENS // rows_blk
    scale = HD ** (-0.5)
    highest = lax.Precision.HIGHEST
    key_pos = jnp.arange(TOKENS, dtype=jnp.int32)

    def per_head(item):
        query_one, key_one, value_one = item

        def per_block(index):
            first_row = (index * rows_blk).astype(jnp.int32)
            query_blk = lax.dynamic_slice_in_dim(query_one, first_row, rows_blk, 0)
            logits = jnp.einsum('igd,jd->gij', query_blk.astype(jnp.float32), key_one.astype(jnp.float32), precision=highest) * scale
            query_pos = first_row + jnp.arange(rows_blk, dtype=jnp.int32)
            allowed = key_pos[None, :] <= query_pos[:, None]
            peak = lax.optimization_barrier(jnp.max(jnp.where(allowed, logits, -jnp.inf), axis=-1))
            probs = jnp.where(allowed, jnp.exp(logits - peak[:, :, None]), 0.0)
            total = lax.optimization_barrier(jnp.sum(probs, axis=-1))
            rounded = lax.optimization_barrier(probs.astype(jnp.bfloat16)).astype(jnp.float32)
            summed = jnp.einsum('gij,jd->igd', rounded, value_one.astype(jnp.float32), precision=highest)
            return (summed / total.T[:, :, None]).astype(jnp.bfloat16)
        return lax.map(per_block, jnp.arange(nquery, dtype=jnp.int32))
    result = lax.map(per_head, (query_heads, key_heads, value_heads))
    return result.transpose(1, 2, 0, 3, 4).reshape(TOKENS, HEADS * HD)

def reference(light_query, light_keys, light_values, log_decay, light_gain, query2, keys2, values2):
    light_out = lightning(light_query, light_keys, light_values, log_decay, light_gain)
    soft_out = softmax_attention_layer(query2, keys2, values2)
    return (light_out, soft_out)
```

```python
import jax
import jax.numpy as jnp
from jax import lax
from jax.experimental import pallas as pl
from jax.experimental.pallas import tpu as pltpu
from jax.sharding import PartitionSpec as P

HEADS = 64
HD = 128
KVH = 8
BLOCK = 256
LOCAL = 4
SHARDS = 32
PIECE = LOCAL * HD // SHARDS
CHUNK = 2048
SCALE = HD**-0.5 * 1.4426950408889634
NEG = -1e30
HUGE = 2.0**100
NT = (((1,), (1,)), ((), ()))
TN = (((0,), (0,)), ((), ()))
f32, bf16 = jnp.float32, jnp.bfloat16


def iota(shape, dim):
    return lax.broadcasted_iota(jnp.int32, shape, dim)


def dot(a, b, dims=(((1,), (0,)), ((), ())), precision=None):
    return lax.dot_general(a, b, dims, precision=precision, preferred_element_type=f32)


def split3(x):
    hi = x.astype(bf16).astype(f32)
    rest = x - hi
    mid = rest.astype(bf16).astype(f32)
    return hi, mid, rest - mid


def pick_kernel(place_ref, keys_ref, values_ref, out_ref):
    out_ref[:, :HD] = keys_ref[...]
    out_ref[:, HD:] = values_ref[...]


def pick(place, keys2, values2):
    rows = keys2.shape[0]
    column = pl.BlockSpec((rows, HD), lambda i, place: (0, place[1] // 2))
    return pl.pallas_call(
        pick_kernel,
        out_shape=jax.ShapeDtypeStruct((rows, 2 * HD), bf16),
        grid_spec=pltpu.PrefetchScalarGridSpec(
            num_scalar_prefetch=1,
            grid=(1,),
            in_specs=[column, column],
            out_specs=pl.BlockSpec((rows, 2 * HD), lambda i, place: (0, 0)),
        ),
        name="pick",
    )(place, keys2, values2)


def decay_columns(decay):
    lower = (iota((BLOCK, BLOCK), 1) <= iota((BLOCK, BLOCK), 0)).astype(f32)
    return dot(lower, decay, NT, lax.Precision.HIGHEST)


def state_kernel(keys_ref, values_ref, decay_ref, out_ref):
    running = decay_columns(decay_ref[...])
    last = running[BLOCK - 1 : BLOCK, :]
    tail = jnp.exp(last - running)
    parts = HD // PIECE
    for h in range(LOCAL):
        cols = slice(h * HD, (h + 1) * HD)
        scaled = (keys_ref[:, cols].astype(f32) * tail[:, h : h + 1]).astype(bf16)
        state = dot(scaled, values_ref[:, cols], TN).astype(bf16)
        hi, mid, lo = split3(last[:, h : h + 1])
        row = iota((PIECE, HD), 0)
        told = jnp.where(row == 0, hi, jnp.where(row == 1, mid, lo)).astype(bf16)
        for i in range(parts):
            out_ref[h * parts + i, :PIECE, :] = state[i * PIECE : (i + 1) * PIECE, :]
            out_ref[h * parts + i, PIECE:, :] = told


def scan_kernel(in_ref, out_ref):
    state = jnp.zeros((PIECE, HD), f32)
    for s in range(SHARDS):
        out_ref[s] = state.astype(bf16)
        told = in_ref[s, PIECE:, :].astype(f32)
        total = told[0:1] + told[1:2] + told[2:3]
        state = jnp.exp(total) * state + in_ref[s, :PIECE, :].astype(f32)


def mix_kernel(query_ref, keys_ref, values_ref, decay_ref, state_ref, gain_ref, out_ref):
    decay = decay_ref[...]
    running = decay_columns(decay)
    upper = (iota((BLOCK, BLOCK), 0) <= iota((BLOCK, BLOCK), 1)).astype(f32)
    along = dot(decay, upper, precision=lax.Precision.HIGHEST)
    grow = jnp.exp(running)
    lower = iota((BLOCK, BLOCK), 1) <= iota((BLOCK, BLOCK), 0)
    for h in range(LOCAL):
        cols = slice(h * HD, (h + 1) * HD)
        query = query_ref[:, cols]
        spread = jnp.where(lower, running[:, h : h + 1] - along[h : h + 1, :], NEG)
        weighted = (dot(query, keys_ref[:, cols], NT) * jnp.exp(spread)).astype(bf16)
        lifted = query.astype(f32) * grow[:, h : h + 1]
        high = lifted.astype(bf16)
        low = (lifted - high.astype(f32)).astype(bf16)
        state = state_ref[h * HD : (h + 1) * HD, :]
        mixed = dot(weighted, values_ref[:, cols]) + dot(high, state) + dot(low, state)
        norm = lax.rsqrt(jnp.mean(mixed * mixed, axis=-1, keepdims=True) + 1e-06)
        out_ref[:, cols] = (mixed * norm * gain_ref[:, cols]).astype(bf16)


def lightning(query, keys, values, decay, gain):
    sent = pl.pallas_call(
        state_kernel,
        out_shape=jax.ShapeDtypeStruct((SHARDS, 2 * PIECE, HD), bf16),
        name="block_state",
    )(keys, values, decay)
    pieces = lax.all_to_all(sent, "seq", 0, 0)
    before = pl.pallas_call(
        scan_kernel,
        out_shape=jax.ShapeDtypeStruct((SHARDS, PIECE, HD), bf16),
        name="state_scan",
    )(pieces)
    state = lax.all_to_all(before, "seq", 0, 0).reshape(LOCAL * HD, HD)
    return pl.pallas_call(
        mix_kernel,
        out_shape=jax.ShapeDtypeStruct(query.shape, bf16),
        name="mix",
    )(query, keys, values, decay, state, gain.reshape(1, LOCAL * HD))


def own_kernel(query_ref, kv_ref, wide_ref, sums_ref):
    keys = kv_ref[:, :HD]
    values = jnp.concatenate([kv_ref[:, HD:], jnp.ones((BLOCK, HD), bf16)], 1)
    allowed = iota((BLOCK, BLOCK), 1) <= iota((BLOCK, BLOCK), 0)
    col = iota((BLOCK, HD), 1)
    for h in range(LOCAL):
        rows = slice(h * BLOCK, (h + 1) * BLOCK)
        query = query_ref[:, h * HD : (h + 1) * HD]
        logits = jnp.where(allowed, dot(query, keys, NT), NEG)
        peak = jnp.max(logits, axis=1, keepdims=True)
        probs = jnp.exp2((logits - peak) * SCALE).astype(bf16)
        sums_ref[rows, :] = dot(probs, values)
        hi, mid, lo = split3(-peak)
        extra = jnp.where(col == 0, hi, jnp.where(col == 1, mid, jnp.where(col == 2, lo, 0.0)))
        extra = jnp.where(col == 3, 1.0, extra)
        wide_ref[rows, :] = jnp.concatenate([query, extra.astype(bf16)], 1)


def attend_kernel(place_ref, wide_ref, first_ref, kv_ref, all_ref, out_ref, sums_ref, held_ref):
    step = pl.program_id(0)
    shard = place_ref[0]
    limit = shard * BLOCK

    @pl.when(step == 0)
    def _():
        sums_ref[...] = first_ref[...]

    @pl.when(step * CHUNK < limit)
    def _():
        col = iota((CHUNK, HD), 1)
        late = iota((CHUNK, HD), 0) + step * CHUNK >= limit
        extra = jnp.where(col < 3, 1.0, jnp.where((col == 3) & late, NEG, 0.0)).astype(bf16)
        keys = jnp.concatenate([kv_ref[:, :HD], extra], 1)
        values = jnp.concatenate([kv_ref[:, HD:], jnp.ones((CHUNK, HD), bf16)], 1)

        def logits(h):
            return dot(wide_ref[h * BLOCK : (h + 1) * BLOCK, :], keys, NT)

        ahead = logits(0)
        probs = None
        for h in range(LOCAL + 1):
            after = logits(h + 1) if h + 1 < LOCAL else None
            if probs is not None:
                sums_ref[(h - 1) * BLOCK : h * BLOCK, :] += dot(probs, values)
            if h < LOCAL:
                probs = jnp.exp2(ahead * SCALE).astype(bf16)
            ahead = after

    @pl.when(step == pl.num_programs(0) - 1)
    def _():
        biggest = jnp.max(sums_ref[:, HD:])
        fine = biggest < HUGE

        @pl.when(fine)
        def _():
            for h in range(LOCAL):
                sums = sums_ref[h * BLOCK : (h + 1) * BLOCK, :]
                out_ref[:, h * HD : (h + 1) * HD] = (sums[:, :HD] / sums[:, HD:]).astype(bf16)

        @pl.when(jnp.logical_not(fine))
        def _():
            row = iota((BLOCK, BLOCK), 0)
            col = iota((BLOCK, BLOCK), 1)
            for h in range(LOCAL):
                rows = slice(h * BLOCK, (h + 1) * BLOCK)
                query = wide_ref[rows, :HD]

                def one(j, carry):
                    peak, total, summed = carry
                    pltpu.sync_copy(all_ref.at[pl.ds(j * BLOCK, BLOCK), :], held_ref)
                    scores = dot(query, held_ref[:, :HD], NT) * SCALE
                    allowed = j * BLOCK + col <= limit + row
                    scores = jnp.where(allowed, scores, NEG)
                    top = jnp.maximum(peak, jnp.max(scores, axis=1, keepdims=True))
                    probs = jnp.where(allowed, jnp.exp2(scores - top), 0.0)
                    factor = jnp.exp2(peak - top)
                    total = factor * total + jnp.sum(probs, axis=1, keepdims=True)
                    summed = factor * summed + dot(probs.astype(bf16), held_ref[:, HD:])
                    return top, total, summed

                start = (
                    jnp.full((BLOCK, 1), NEG, f32),
                    jnp.zeros((BLOCK, 1), f32),
                    jnp.zeros((BLOCK, HD), f32),
                )
                _, total, summed = lax.fori_loop(0, shard + 1, one, start)
                out_ref[:, h * HD : (h + 1) * HD] = (summed / total).astype(bf16)


def attention(place, query, kv, gathered):
    rows = LOCAL * BLOCK
    wide, first = pl.pallas_call(
        own_kernel,
        out_shape=[
            jax.ShapeDtypeStruct((rows, 2 * HD), bf16),
            jax.ShapeDtypeStruct((rows, 2 * HD), f32),
        ],
        name="own_block",
    )(query, kv)
    steps = gathered.shape[0] // CHUNK
    whole = pl.BlockSpec((rows, 2 * HD), lambda j, place: (0, 0))

    def needed(j, place):
        return (jnp.minimum(j, jnp.maximum(place[0] * BLOCK - 1, 0) // CHUNK), 0)

    return pl.pallas_call(
        attend_kernel,
        out_shape=jax.ShapeDtypeStruct(query.shape, bf16),
        grid_spec=pltpu.PrefetchScalarGridSpec(
            num_scalar_prefetch=1,
            grid=(steps,),
            in_specs=[
                whole,
                whole,
                pl.BlockSpec((CHUNK, 2 * HD), needed),
                pl.BlockSpec(memory_space=pl.ANY),
            ],
            out_specs=pl.BlockSpec(query.shape, lambda j, place: (0, 0)),
            scratch_shapes=[pltpu.VMEM((rows, 2 * HD), f32), pltpu.VMEM((BLOCK, 2 * HD), bf16)],
        ),
        compiler_params=pltpu.CompilerParams(vmem_limit_bytes=48 * 2**20),
        name="attend",
    )(place, wide, first, gathered, gathered)


def local(light_query, light_keys, light_values, log_decay, light_gain, query2, keys2, values2):
    place = jnp.stack([lax.axis_index("seq"), lax.axis_index("head")]).astype(jnp.int32)
    kv = pick(place, keys2, values2)
    gathered = lax.all_gather(kv, "seq", axis=0, tiled=True)
    light_out = lightning(light_query, light_keys, light_values, log_decay, light_gain)
    soft_out = attention(place, query2, kv, gathered)
    return (light_out, soft_out)


def solution(mesh):
    placed = (
        P("seq", "head"),
        P("seq", "head"),
        P("seq", "head"),
        P("head", "seq"),
        P("head"),
        P("seq", "head"),
        P("seq", None),
        P("seq", None),
    )
    return jax.shard_map(
        local,
        mesh=mesh,
        in_specs=placed,
        out_specs=(P("seq", "head"), P("seq", "head")),
        check_vma=False,
    )
```

```python
import jax
import jax.numpy as jnp
from jax import lax
from jax.experimental import pallas as pl
from jax.experimental.pallas import tpu as pltpu
from jax.sharding import PartitionSpec as P

HEADS = 64
HD = 128
KVH = 8
BLOCK = 256
CHIPS = 16
LOCAL = 4
HALF = LOCAL // 2
ROWS = LOCAL * BLOCK
SHARE = BLOCK // 2
SCALE = HD**-0.5 * 1.4426950408889634
NEG = -1e30
HUGE = 2.0**100
NT = (((1,), (1,)), ((), ()))
TN = (((0,), (0,)), ((), ()))
f32, bf16 = jnp.float32, jnp.bfloat16

FAR = (
    [(z, z + 4) for z in range(12)],
    [(z, z + 8) for z in range(8)],
    [(z, z + 12) for z in range(4)],
)
FIFTH = (
    [(z, z + 5) for z in range(11)] + [(11, 0), (12, 1)],
    [(z, z + 10) for z in range(6)] + [(6, 0), (7, 1)],
    [(0, 15), (1, 0), (2, 1)],
)
NEAR = [[(z, z + d) for z in range(CHIPS - d)] for d in (1, 2)]
UP1 = [(z, z + 1) for z in range(15)]
UP2 = [(z, z + 2) for z in range(14)]
DOWN1 = [(z, z - 1) for z in range(5, 16)] + [(0, 15)]
DOWN2 = [(z, z - 2) for z in range(5, 16)] + [(0, 14), (1, 15)]


def on_core(core, chips):
    return [(2 * a + core, 2 * b + core) for a, b in chips]


def on_both(chips):
    return on_core(0, chips) + on_core(1, chips)


PAIRS = [[s, s + 1] for s in range(0, 2 * CHIPS, 2)]
SWAP = [(s, s ^ 1) for s in range(2 * CHIPS)]
MATES = [(h, h ^ 1) for h in range(16)]


def iota(shape, dim):
    return lax.broadcasted_iota(jnp.int32, shape, dim)


def dot(a, b, dims=(((1,), (0,)), ((), ())), precision=None):
    return lax.dot_general(a, b, dims, precision=precision, preferred_element_type=f32)


def split3(x):
    hi = x.astype(bf16).astype(f32)
    rest = x - hi
    mid = rest.astype(bf16).astype(f32)
    return hi, mid, rest - mid


def shape(*dims, dtype=f32):
    return jax.ShapeDtypeStruct(dims, dtype)


def call(kernel, out_shape, place, *args, left=0, scratch=(), name=None, flops=0, limit=16):
    def spec(dims):
        return pl.BlockSpec(dims, lambda i, place: (0,) * len(dims))

    many = isinstance(out_shape, list)
    outs = out_shape if many else [out_shape]
    specs = [spec(a.shape) for a in args]
    if left:
        specs[-left:] = [pl.BlockSpec(memory_space=pl.ANY)] * left
    out_specs = [spec(o.shape) for o in outs]
    return pl.pallas_call(
        kernel,
        out_shape=out_shape,
        grid_spec=pltpu.PrefetchScalarGridSpec(
            num_scalar_prefetch=1,
            grid=(1,),
            in_specs=specs,
            out_specs=out_specs if many else out_specs[0],
            scratch_shapes=scratch,
        ),
        compiler_params=pltpu.CompilerParams(vmem_limit_bytes=limit * 2**20),
        cost_estimate=pl.CostEstimate(
            flops=flops, bytes_accessed=sum(a.size * a.dtype.itemsize for a in args), transcendentals=0
        ),
        name=name,
    )(place, *args)


def pick_kernel(place_ref, keys_ref, values_ref, out_ref, share_ref):
    out_ref[:, :HD] = keys_ref[...]
    out_ref[:, HD:] = values_ref[...]
    start = pl.multiple_of(place_ref[1] % 2 * SHARE, SHARE)
    share_ref[...] = out_ref[pl.ds(start, SHARE), :]


def pick(place, keys2, values2):
    column = pl.BlockSpec((BLOCK, HD), lambda i, place: (0, place[1] // 2))
    return pl.pallas_call(
        pick_kernel,
        out_shape=[shape(BLOCK, 2 * HD, dtype=bf16), shape(SHARE, 2 * HD, dtype=bf16)],
        grid_spec=pltpu.PrefetchScalarGridSpec(
            num_scalar_prefetch=1,
            grid=(1,),
            in_specs=[column, column],
            out_specs=[
                pl.BlockSpec((BLOCK, 2 * HD), lambda i, place: (0, 0)),
                pl.BlockSpec((SHARE, 2 * HD), lambda i, place: (0, 0)),
            ],
        ),
        name="pick",
    )(place, keys2, values2)


STATE = LOCAL * HD
CARRIED = HALF * HD
TAIL = 16


def decay_columns(decay):
    lower = (iota((BLOCK, BLOCK), 1) <= iota((BLOCK, BLOCK), 0)).astype(f32)
    return dot(lower, decay, NT, lax.Precision.HIGHEST)


def told_rows(columns):
    lane, row = iota((TAIL, HD), 1), iota((TAIL, HD), 0)
    out = jnp.zeros((TAIL, HD), f32)
    for h, value in enumerate(columns):
        hi, mid, lo = split3(value)
        parts = jnp.where(row == 0, hi, jnp.where(row == 1, mid, jnp.where(row == 2, lo, 0.0)))
        out = jnp.where(lane == h, parts, out)
    return out.astype(bf16)


def told(rows):
    return jnp.sum(rows.astype(f32), axis=0, keepdims=True)


def state_kernel(keys_ref, values_ref, decay_ref, out_ref):
    running = decay_columns(decay_ref[...])
    last = running[BLOCK - 1 : BLOCK, :]
    tail = jnp.exp(last - running)
    for h in range(LOCAL):
        cols = slice(h * HD, (h + 1) * HD)
        scaled = (keys_ref[:, cols].astype(f32) * tail[:, h : h + 1]).astype(bf16)
        out_ref[cols, :] = dot(scaled, values_ref[:, cols], TN).astype(bf16)
    out_ref[STATE:, :] = told_rows([last[:, h : h + 1] for h in range(LOCAL)])


def chip_kernel(place_ref, both_ref, out_ref):
    core = place_ref[0] % 2
    size = STATE + TAIL
    first, second = told(both_ref[STATE:size, :]), told(both_ref[size + STATE :, :])
    sums = []
    for i in range(HALF):
        start = pl.multiple_of((core * HALF + i) * HD, HD)

        def head(row):
            return jnp.where(core == 0, row[:, i : i + 1], row[:, HALF + i : HALF + i + 1])

        later = head(second)
        state = jnp.exp(later) * both_ref[pl.ds(start, HD), :].astype(f32)
        state = state + both_ref[pl.ds(size + start, HD), :].astype(f32)
        out_ref[i * HD : (i + 1) * HD, :] = state.astype(bf16)
        sums.append(head(first) + later)
    out_ref[CARRIED:, :] = told_rows(sums)


def chain(refs):
    states, total = [], None
    decays = [told(ref[CARRIED:, :]) for ref in refs]
    for i in range(HALF):
        rows = slice(i * HD, (i + 1) * HD)
        state = refs[-1][rows, :].astype(f32)
        for ref, decay in zip(refs[-2::-1], decays[-2::-1]):
            state = ref[rows, :].astype(f32) + jnp.exp(decay[:, i : i + 1]) * state
        states.append(state)
    total = sum(decays[1:], decays[0])
    return states, total


def window_kernel(*refs):
    out_ref = refs[-1]
    states, total = chain(refs[:-1])
    for i, state in enumerate(states):
        out_ref[i * HD : (i + 1) * HD, :] = state.astype(bf16)
    out_ref[CARRIED:, :] = told_rows([total[:, i : i + 1] for i in range(HALF)])


def before_kernel(near1_ref, near2_ref, far1_ref, far2_ref, far3_ref, out_ref):
    near, decay = chain([near1_ref, near2_ref])
    far, _ = chain([far1_ref, far2_ref, far3_ref])
    for i in range(HALF):
        state = near[i] + jnp.exp(decay[:, i : i + 1]) * far[i]
        out_ref[i * HD : (i + 1) * HD, :] = state.astype(bf16)


def mix_kernel(
    place_ref, query_ref, keys_ref, values_ref, decay_ref, gain_ref, both_ref, before_ref, out_ref
):
    core = place_ref[0] % 2
    decay = decay_ref[...]
    running = decay_columns(decay)
    upper = (iota((BLOCK, BLOCK), 0) <= iota((BLOCK, BLOCK), 1)).astype(f32)
    along = dot(decay, upper, precision=lax.Precision.HIGHEST)
    grow = jnp.exp(running)
    lower = iota((BLOCK, BLOCK), 1) <= iota((BLOCK, BLOCK), 0)
    first = jnp.exp(told(both_ref[STATE : STATE + TAIL, :]))
    for h in range(LOCAL):
        cols = slice(h * HD, (h + 1) * HD)
        query = query_ref[:, cols]
        spread = jnp.where(lower, running[:, h : h + 1] - along[h : h + 1, :], NEG)
        weighted = (dot(query, keys_ref[:, cols], NT) * jnp.exp(spread)).astype(bf16)
        lifted = query.astype(f32) * grow[:, h : h + 1]
        high = lifted.astype(bf16)
        low = (lifted - high.astype(f32)).astype(bf16)
        state = before_ref[cols, :].astype(f32)
        after = first[:, h : h + 1] * state + both_ref[cols, :].astype(f32)
        state = jnp.where(core == 0, state, after).astype(bf16)
        mixed = dot(weighted, values_ref[:, cols]) + dot(high, state) + dot(low, state)
        norm = lax.rsqrt(jnp.mean(mixed * mixed, axis=-1, keepdims=True) + 1e-06)
        out_ref[:, cols] = (mixed * norm * gain_ref[:, cols]).astype(bf16)


def chip_states(place, keys, values, decay):
    mine = pl.pallas_call(state_kernel, out_shape=shape(STATE + TAIL, HD, dtype=bf16), name="block_state")(
        keys, values, decay
    )
    both = lax.all_gather(mine, "seq", axis=0, tiled=True, axis_index_groups=PAIRS)
    carried = shape(CARRIED + TAIL, HD, dtype=bf16)
    chip = call(chip_kernel, carried, place, both, name="chip_state")
    below = lax.ppermute(chip, "seq", on_both(NEAR[0]))
    return both, chip, below


def windows(chip, below):
    def window(*parts):
        out = shape(CARRIED + TAIL, HD, dtype=bf16)
        return pl.pallas_call(window_kernel, out_shape=out, name="window_state")(*parts)

    below2 = lax.ppermute(window(chip, below), "seq", on_both(NEAR[1]))
    return [below, below2], window(chip, below, below2)


def mixed(place, query, keys, values, decay, gain, both, near, window, after):
    far = [lax.ppermute(window, "seq", on_both(pairs)) for pairs in FAR]
    far, _ = lax.optimization_barrier((far, after))
    before = pl.pallas_call(before_kernel, out_shape=shape(CARRIED, HD, dtype=bf16), name="state_before")(
        *near, *far
    )
    before = lax.all_gather(before, "seq", axis=0, tiled=True, axis_index_groups=PAIRS)
    gain = gain.reshape(1, LOCAL * HD)
    out = shape(*query.shape, dtype=bf16)
    return call(mix_kernel, out, place, query, keys, values, decay, gain, both, before, name="mix")


FAR_BLOCKS = tuple((4 * core + i, 5 * i) for core in (0, 1) for i in (1, 2, 3))


def near_blocks(core):
    out = []
    for side in range(2):
        for hops in (1, 2):
            first = jnp.where(core == side, hops, 5 - hops)
            out += [first + 5 * i for both in range(2) for i in range(3)]
    return out


def attend(wide_ref, sums_ref, blocks):
    col = iota((SHARE, HD), 1)
    counts = jnp.where(col < 3, 1.0, 0.0)
    misses = jnp.where(col < 3, 1.0, jnp.where(col == 3, NEG, 0.0))
    extra = jnp.concatenate([jnp.where(ok, counts, misses).astype(bf16) for _, ok in blocks], 0)
    kv = jnp.concatenate([rows for rows, _ in blocks], 0)
    keys = jnp.concatenate([kv[:, :HD], extra], 1)
    values = jnp.concatenate([kv[:, HD:], jnp.ones(extra.shape, bf16)], 1)
    tiles = sums_ref.shape[0] // BLOCK

    def logits(i):
        return dot(wide_ref[i * BLOCK : (i + 1) * BLOCK, :], keys, NT)

    ahead = logits(0)
    probs = None
    for i in range(tiles + 1):
        after = logits(i + 1) if i + 1 < tiles else None
        if probs is not None:
            sums_ref[(i - 1) * BLOCK : i * BLOCK, :] += dot(probs, values)
        if i < tiles:
            probs = jnp.exp2(ahead * SCALE).astype(bf16)
        ahead = after


def rows_of(ref, block):
    return ref[block * SHARE : (block + 1) * SHARE, :]


def near_kernel(place_ref, query_ref, mate_ref, kv_ref, far_ref, wide_ref, sums_ref):
    core, chip = place_ref[0] % 2, place_ref[0] // 2
    keys = kv_ref[:, :HD]
    values = jnp.concatenate([kv_ref[:, HD:], jnp.ones((BLOCK, HD), bf16)], 1)
    col = iota((BLOCK, HD), 1)
    allowed = iota((BLOCK, BLOCK), 1) <= iota((BLOCK, BLOCK), 0)
    for side, ref in enumerate((query_ref, mate_ref)):
        for h in range(LOCAL):
            rows = slice(side * ROWS + h * BLOCK, side * ROWS + (h + 1) * BLOCK)
            query = ref[:, h * HD : (h + 1) * HD]
            logits = jnp.where(allowed, dot(query, keys, NT), NEG)
            peak = jnp.max(logits, axis=1, keepdims=True)
            if side == 0:
                probs = jnp.exp2((logits - peak) * SCALE).astype(bf16)
                sums_ref[rows, :] = dot(probs, values)
            else:
                sums_ref[rows, :] = jnp.zeros((BLOCK, 2 * HD), f32)
            hi, mid, lo = split3(-peak)
            extra = jnp.where(col == 0, hi, jnp.where(col == 1, mid, jnp.where(col == 2, lo, 0.0)))
            extra = jnp.where(col == 3, 1.0, extra)
            wide_ref[rows, :] = jnp.concatenate([query, extra.astype(bf16)], 1)

    @pl.when((chip >= 5) | (core == 1))
    def _():
        blocks = [(rows_of(far_ref, 0), core == 1)]
        attend(wide_ref, sums_ref, blocks + [(rows_of(far_ref, i), chip >= d) for i, d in FAR_BLOCKS])


def rest_kernel(diagonal, place_ref, wide_ref, sums_in_ref, *refs):
    near_refs = refs[:4]
    kv_ref, far_ref, out_ref, sums_ref, peak_ref, held_ref = refs[4:]
    core, chip = place_ref[0] % 2, place_ref[0] // 2
    distances = near_blocks(core)
    sums_ref[...] = sums_in_ref[...]

    @pl.when(chip >= 1)
    def _():
        attend(
            wide_ref,
            sums_ref,
            [(rows_of(near_refs[i // 6], i % 6), chip >= d) for i, d in enumerate(distances)],
        )

    minus = jnp.where(iota((HD, HD), 0) < 3, -1.0, 0.0).astype(bf16)
    peak_ref[...] = dot(wide_ref[:, HD:], minus)

    @pl.when(jnp.logical_not(jnp.max(sums_ref[:, HD:]) < HUGE))
    def _():
        @pl.loop(0, LOCAL)
        def _(h):
            rows = pl.ds(pl.multiple_of(h * BLOCK, BLOCK), BLOCK)
            query = wide_ref[rows, :HD]
            whole = jnp.zeros((BLOCK, SHARE), jnp.int32)

            def add(carry, source, i, allowed):
                peak, total, summed = carry
                pltpu.sync_copy(source.at[pl.ds(pl.multiple_of(i * SHARE, SHARE), SHARE), :], held_ref)
                scores = jnp.where(allowed, dot(query, held_ref[:, :HD], NT), NEG)
                top = jnp.maximum(peak, jnp.max(scores, axis=1, keepdims=True))
                probs = jnp.where(allowed, jnp.exp2((scores - top) * SCALE), 0.0)
                factor = jnp.exp2((peak - top) * SCALE)
                total = factor * total + jnp.sum(probs, axis=1, keepdims=True)
                return top, total, factor * summed + dot(probs.astype(bf16), held_ref[:, HD:])

            def diagonal_part(j, carry):
                return add(carry, kv_ref, j, j * SHARE + iota((BLOCK, SHARE), 1) <= iota((BLOCK, SHARE), 0))

            def far_part(j, carry):
                first = jnp.where(core == 1, 0, CHIPS)
                distance = jnp.where(j == 0, first, jnp.where(j == 4, CHIPS, j % 4 * 5))
                return add(carry, far_ref, j, whole + chip >= distance)

            carry = (jnp.full((BLOCK, 1), NEG, f32), jnp.zeros((BLOCK, 1), f32), jnp.zeros((BLOCK, HD), f32))
            if diagonal:
                carry = lax.fori_loop(0, 2, diagonal_part, carry)
            carry = lax.fori_loop(0, 8, far_part, carry)
            for source, ref in enumerate(near_refs):

                def near_part(j, carry):
                    return add(carry, ref, j, whole + chip >= distances[6 * source] + j % 3 * 5)

                carry = lax.fori_loop(0, 6, near_part, carry)
            peak, total, summed = carry
            sums_ref[rows, :] = jnp.concatenate([summed, jnp.broadcast_to(total, (BLOCK, HD))], 1)
            peak_ref[rows, :] = jnp.broadcast_to(peak, (BLOCK, HD))

    lane = iota((BLOCK, HD), 1)
    stats = jnp.zeros((BLOCK, HD), f32)
    for h in range(LOCAL):
        rows = slice(h * BLOCK, (h + 1) * BLOCK)
        out_ref[:, h * HD : (h + 1) * HD] = sums_ref[rows, :HD].astype(out_ref.dtype)
        stats = jnp.where(lane % LOCAL == h, jnp.where(lane < 3 * LOCAL, sums_ref[rows, HD:], peak_ref[rows, :]), stats)
    hi, mid, lo = split3(stats)
    part = lane // LOCAL % 3
    stats = jnp.where(part == 0, hi, jnp.where(part == 1, mid, lo))
    out_ref[:, LOCAL * HD :] = stats.astype(out_ref.dtype)


def merge_kernel(mine_ref, other_ref, out_ref):
    wide = LOCAL * HD
    lane, head = iota((HD, wide), 0), iota((HD, wide), 1) // HD

    def spread(ref, i):
        chosen = (lane // LOCAL // 3 == i) & (lane % LOCAL == head) & (lane < 6 * LOCAL)
        return dot(ref[:, wide:].astype(bf16), jnp.where(chosen, 1.0, 0.0).astype(bf16))

    here, there = spread(mine_ref, 1), spread(other_ref, 1)
    top = jnp.maximum(here, there)
    here, there = jnp.exp2((here - top) * SCALE), jnp.exp2((there - top) * SCALE)
    whole = here * spread(mine_ref, 0) + there * spread(other_ref, 0)
    summed = here * mine_ref[:, :wide].astype(f32) + there * other_ref[:, :wide].astype(f32)
    out_ref[...] = (summed / whole).astype(bf16)


def attention(place, query, kv, share, chip, below):
    brought = [lax.ppermute(share, "seq", on_both(pairs)) for pairs in FIFTH]
    query, _ = lax.optimization_barrier((query, chip))
    mate = lax.ppermute(query, "head", MATES)
    brought, _ = lax.optimization_barrier((jnp.concatenate([share, *brought]), chip))
    far = lax.all_gather(brought, "seq", axis=0, tiled=True, axis_index_groups=PAIRS)
    far, below = lax.optimization_barrier((far, below))
    out = lax.dynamic_slice_in_dim(far.reshape(2, 4 * SHARE, 2 * HD), place[0] % 2 * SHARE, 3 * SHARE, 1)
    out = out.reshape(6 * SHARE, 2 * HD)
    next1 = lax.ppermute(out, "seq", on_core(0, UP1) + on_core(1, DOWN1))
    second1 = lax.ppermute(out, "seq", on_core(0, UP2) + on_core(1, DOWN2))
    near, window = windows(chip, below)
    wide, sums = call(
        near_kernel,
        [shape(2 * ROWS, 2 * HD, dtype=bf16), shape(2 * ROWS, 2 * HD)],
        place,
        query,
        mate,
        kv,
        far,
        name="attend_near",
        limit=32,
        flops=4 * ROWS * 8 * BLOCK * 2 * HD,
    )
    next1, second1, sums, window = lax.optimization_barrier((next1, second1, sums, window))
    next2 = lax.ppermute(next1, "seq", SWAP)
    second2 = lax.ppermute(second1, "seq", SWAP)

    def rest(side, dtype):
        def kernel(*refs):
            rest_kernel(side == 0, *refs)

        return pl.pallas_call(
            kernel,
            out_shape=shape(BLOCK, LOCAL * HD + HD, dtype=dtype),
            grid_spec=pltpu.PrefetchScalarGridSpec(
                num_scalar_prefetch=1,
                grid=(1,),
                in_specs=[pl.BlockSpec((ROWS, 2 * HD), lambda i, place: (side, 0))] * 2
                + [pl.BlockSpec(out.shape, lambda i, place: (0, 0))] * 4
                + [pl.BlockSpec(memory_space=pl.ANY)] * 2,
                out_specs=pl.BlockSpec((BLOCK, LOCAL * HD + HD), lambda i, place: (0, 0)),
                scratch_shapes=[
                    pltpu.VMEM((ROWS, 2 * HD), f32),
                    pltpu.VMEM((ROWS, HD), f32),
                    pltpu.VMEM((SHARE, 2 * HD), bf16),
                ],
            ),
            compiler_params=pltpu.CompilerParams(vmem_limit_bytes=32 * 2**20),
            cost_estimate=pl.CostEstimate(
                flops=4 * ROWS * 12 * BLOCK * 2 * HD, bytes_accessed=2**22, transcendentals=0
            ),
            name="attend_rest",
        )(place, wide, sums, next1, second1, next2, second2, kv, far)

    other = lax.ppermute(rest(1, bf16), "head", MATES)
    mine = rest(0, f32)
    soft_out = pl.pallas_call(merge_kernel, out_shape=shape(*query.shape, dtype=bf16), name="merge")(mine, other)
    return soft_out, window, near, mine


def local(light_query, light_keys, light_values, log_decay, light_gain, query2, keys2, values2):
    place = jnp.stack([lax.axis_index("seq"), lax.axis_index("head")]).astype(jnp.int32)
    kv, share = pick(place, keys2, values2)
    both, chip, below = chip_states(place, light_keys, light_values, log_decay)
    soft_out, window, near, mine = attention(place, query2, kv, share, chip, below)
    light_out = mixed(
        place, light_query, light_keys, light_values, log_decay, light_gain, both, near, window, mine
    )
    return (light_out, soft_out)


def solution(mesh):
    placed = (
        P("seq", "head"),
        P("seq", "head"),
        P("seq", "head"),
        P("head", "seq"),
        P("head"),
        P("seq", "head"),
        P("seq", None),
        P("seq", None),
    )
    return jax.shard_map(
        local,
        mesh=mesh,
        in_specs=placed,
        out_specs=(P("seq", "head"), P("seq", "head")),
        check_vma=False,
    )
```

```python
import jax
import jax.numpy as jnp
from jax import lax
from jax.experimental import pallas as pl
from jax.experimental.pallas import tpu as pltpu
from jax.sharding import PartitionSpec as P

HEADS = 64
HD = 128
KVH = 8
BLOCK = 256
CHIPS = 16
LOCAL = 4
ROWS = LOCAL * BLOCK
SHARE = BLOCK // 2
SCALE = HD**-0.5 * 1.4426950408889634
NEG = -1e30
HUGE = 2.0**100
NT = (((1,), (1,)), ((), ()))
TN = (((0,), (0,)), ((), ()))
f32, bf16 = jnp.float32, jnp.bfloat16

def below(distance):
    return [(z, z + distance) for z in range(CHIPS - distance)]


FIVE = below(5) + [(11, 0), (12, 1)]
TEN = below(10) + [(6, 0), (7, 1)]
FIFTEEN = below(15) + [(1, 0), (2, 1)]
UP1 = [(z, z + 1) for z in range(15)]
UP2 = [(z, z + 2) for z in range(14)]
DOWN1 = [(z, z - 1) for z in range(5, 16)] + [(0, 15)]
DOWN2 = [(z, z - 2) for z in range(5, 16)] + [(0, 14), (1, 15)]


def on_core(core, chips):
    return [(2 * a + core, 2 * b + core) for a, b in chips]


PAIRS = [[s, s + 1] for s in range(0, 2 * CHIPS, 2)]
SWAP = [(s, s ^ 1) for s in range(2 * CHIPS)]
MATES = [(h, h ^ 1) for h in range(16)]


def iota(shape, dim):
    return lax.broadcasted_iota(jnp.int32, shape, dim)


def dot(a, b, dims=(((1,), (0,)), ((), ())), precision=None):
    return lax.dot_general(a, b, dims, precision=precision, preferred_element_type=f32)


def after(*values):
    return lax.optimization_barrier(values)


def split3(x):
    hi = x.astype(bf16).astype(f32)
    rest = x - hi
    mid = rest.astype(bf16).astype(f32)
    return hi, mid, rest - mid


def shape(*dims, dtype=f32):
    return jax.ShapeDtypeStruct(dims, dtype)


def call(kernel, out_shape, place, *args, left=0, scratch=(), name=None, flops=0, limit=16):
    def spec(dims):
        return pl.BlockSpec(dims, lambda i, place: (0,) * len(dims))

    many = isinstance(out_shape, list)
    outs = out_shape if many else [out_shape]
    specs = [spec(a.shape) for a in args]
    if left:
        specs[-left:] = [pl.BlockSpec(memory_space=pl.ANY)] * left
    out_specs = [spec(o.shape) for o in outs]
    return pl.pallas_call(
        kernel,
        out_shape=out_shape,
        grid_spec=pltpu.PrefetchScalarGridSpec(
            num_scalar_prefetch=1,
            grid=(1,),
            in_specs=specs,
            out_specs=out_specs if many else out_specs[0],
            scratch_shapes=scratch,
        ),
        compiler_params=pltpu.CompilerParams(vmem_limit_bytes=limit * 2**20),
        cost_estimate=pl.CostEstimate(
            flops=flops, bytes_accessed=sum(a.size * a.dtype.itemsize for a in args), transcendentals=0
        ),
        name=name,
    )(place, *args)


def pick_kernel(place_ref, keys_ref, values_ref, out_ref, share_ref):
    out_ref[:, :HD] = keys_ref[...]
    out_ref[:, HD:] = values_ref[...]
    start = pl.multiple_of(place_ref[1] % 2 * SHARE, SHARE)
    share_ref[...] = out_ref[pl.ds(start, SHARE), :]


def pick(place, keys2, values2):
    column = pl.BlockSpec((BLOCK, HD), lambda i, place: (0, place[1] // 2))
    return pl.pallas_call(
        pick_kernel,
        out_shape=[shape(BLOCK, 2 * HD, dtype=bf16), shape(SHARE, 2 * HD, dtype=bf16)],
        grid_spec=pltpu.PrefetchScalarGridSpec(
            num_scalar_prefetch=1,
            grid=(1,),
            in_specs=[column, column],
            out_specs=[
                pl.BlockSpec((BLOCK, 2 * HD), lambda i, place: (0, 0)),
                pl.BlockSpec((SHARE, 2 * HD), lambda i, place: (0, 0)),
            ],
        ),
        name="pick",
    )(place, keys2, values2)


STATE = LOCAL * HD
TAIL = 16
SENT = STATE + TAIL


def decay_columns(decay):
    lower = (iota((BLOCK, BLOCK), 1) <= iota((BLOCK, BLOCK), 0)).astype(f32)
    return dot(lower, decay, NT, lax.Precision.HIGHEST)


def told_rows(columns):
    lane, row = iota((TAIL, HD), 1), iota((TAIL, HD), 0)
    out = jnp.zeros((TAIL, HD), f32)
    for h, value in enumerate(columns):
        hi, mid, lo = split3(value)
        parts = jnp.where(row == 0, hi, jnp.where(row == 1, mid, jnp.where(row == 2, lo, 0.0)))
        out = jnp.where(lane == h, parts, out)
    return out.astype(bf16)


def told(rows):
    return jnp.sum(rows.astype(f32), axis=0, keepdims=True)


def state_kernel(keys_ref, values_ref, decay_ref, out_ref):
    running = decay_columns(decay_ref[...])
    last = running[BLOCK - 1 : BLOCK, :]
    tail = jnp.exp(last - running)
    for h in range(LOCAL):
        cols = slice(h * HD, (h + 1) * HD)
        scaled = (keys_ref[:, cols].astype(f32) * tail[:, h : h + 1]).astype(bf16)
        out_ref[cols, :] = dot(scaled, values_ref[:, cols], TN).astype(bf16)
    out_ref[STATE:, :] = told_rows([last[:, h : h + 1] for h in range(LOCAL)])


def chain(parts):
    decays = [told(part[STATE:, :]) for part in parts]

    def state(h):
        rows = slice(h * HD, (h + 1) * HD)
        out = parts[-1][rows, :].astype(f32)
        for part, decay in zip(parts[-2::-1], decays[-2::-1]):
            out = part[rows, :].astype(f32) + jnp.exp(decay[:, h : h + 1]) * out
        return out

    return state, sum(decays[1:], decays[0])


def chain_kernel(order, *refs):
    out_ref = refs[-1]
    state, total = chain([refs[i].at[j * SENT : (j + 1) * SENT] for i, j in order])
    for h in range(LOCAL):
        out_ref[h * HD : (h + 1) * HD, :] = state(h).astype(bf16)
    out_ref[STATE:, :] = told_rows([total[:, h : h + 1] for h in range(LOCAL)])


def chained(name, order, *arrays):
    def kernel(*refs):
        chain_kernel(order, *refs)

    return pl.pallas_call(kernel, out_shape=shape(SENT, HD, dtype=bf16), name=name)(*arrays)


JOINED = (0, 2, 1)


def join(first, second):
    return lax.all_gather(
        jnp.concatenate([first, second]), "seq", axis=0, tiled=True, axis_index_groups=PAIRS
    )


def mix_kernel(
    place_ref, query_ref, keys_ref, values_ref, decay_ref, gain_ref, both_ref, near_ref, far_ref, out_ref
):
    core = place_ref[0] % 2
    decay = decay_ref[...]
    running = decay_columns(decay)
    upper = (iota((BLOCK, BLOCK), 0) <= iota((BLOCK, BLOCK), 1)).astype(f32)
    along = dot(decay, upper, precision=lax.Precision.HIGHEST)
    grow = jnp.exp(running)
    lower = iota((BLOCK, BLOCK), 1) <= iota((BLOCK, BLOCK), 0)
    first = jnp.exp(told(both_ref[STATE:SENT, :]))
    near, decays = chain([near_ref.at[j * SENT : (j + 1) * SENT] for j in JOINED])
    far, _ = chain([far_ref.at[j * SENT : (j + 1) * SENT] for j in JOINED])
    for h in range(LOCAL):
        cols = slice(h * HD, (h + 1) * HD)
        query = query_ref[:, cols]
        spread = jnp.where(lower, running[:, h : h + 1] - along[h : h + 1, :], NEG)
        weighted = (dot(query, keys_ref[:, cols], NT) * jnp.exp(spread)).astype(bf16)
        lifted = query.astype(f32) * grow[:, h : h + 1]
        high = lifted.astype(bf16)
        low = (lifted - high.astype(f32)).astype(bf16)
        state = near(h) + jnp.exp(decays[:, h : h + 1]) * far(h)
        after = first[:, h : h + 1] * state + both_ref[cols, :].astype(f32)
        state = jnp.where(core == 0, state, after).astype(bf16)
        mixed = dot(weighted, values_ref[:, cols]) + dot(high, state) + dot(low, state)
        norm = lax.rsqrt(jnp.mean(mixed * mixed, axis=-1, keepdims=True) + 1e-06)
        out_ref[:, cols] = (mixed * norm * gain_ref[:, cols]).astype(bf16)


def chip_states(keys, values, decay):
    mine = pl.pallas_call(state_kernel, out_shape=shape(SENT, HD, dtype=bf16), name="block_state")(
        keys, values, decay
    )
    both = lax.all_gather(mine, "seq", axis=0, tiled=True, axis_index_groups=PAIRS)
    return both, chained("chip_state", [(0, 1), (0, 0)], both)


def bring(state, distances):
    first, second, third = distances
    return (
        lax.ppermute(state, "seq", on_core(0, below(first)) + on_core(1, below(second))),
        lax.ppermute(state, "seq", on_core(0, below(third))),
    )


FAR_BLOCKS = tuple((i, 15 - 5 * (i // 2)) for i in range(6))


def near_blocks(core):
    out = []
    for side in range(2):
        for hops in (1, 2):
            first = jnp.where(core == side, 10 + hops, 15 - hops)
            out += [first - 5 * (i // 2) for i in range(6)]
    return out


def attend(wide_ref, sums_ref, blocks):
    col = iota((SHARE, HD), 1)
    counts = jnp.where(col < 3, 1.0, 0.0)
    misses = jnp.where(col < 3, 1.0, jnp.where(col == 3, NEG, 0.0))
    extra = jnp.concatenate([jnp.where(ok, counts, misses).astype(bf16) for _, ok in blocks], 0)
    kv = jnp.concatenate([rows for rows, _ in blocks], 0)
    keys = jnp.concatenate([kv[:, :HD], extra], 1)
    values = jnp.concatenate([kv[:, HD:], jnp.ones(extra.shape, bf16)], 1)
    tiles = sums_ref.shape[0] // BLOCK

    def logits(i):
        return dot(wide_ref[i * BLOCK : (i + 1) * BLOCK, :], keys, NT)

    ahead = logits(0)
    probs = None
    for i in range(tiles + 1):
        after = logits(i + 1) if i + 1 < tiles else None
        if probs is not None:
            sums_ref[(i - 1) * BLOCK : i * BLOCK, :] += dot(probs, values)
        if i < tiles:
            probs = jnp.exp2(ahead * SCALE).astype(bf16)
        ahead = after


def rows_of(ref, block):
    return ref[block * SHARE : (block + 1) * SHARE, :]


def near_kernel(place_ref, query_ref, mate_ref, kv_ref, far_ref, wide_ref, sums_ref):
    core, chip = place_ref[0] % 2, place_ref[0] // 2
    keys = kv_ref[:, :HD]
    values = jnp.concatenate([kv_ref[:, HD:], jnp.ones((BLOCK, HD), bf16)], 1)
    col = iota((BLOCK, HD), 1)
    allowed = iota((BLOCK, BLOCK), 1) <= iota((BLOCK, BLOCK), 0)
    for side, ref in enumerate((query_ref, mate_ref)):
        for h in range(LOCAL):
            rows = slice(side * ROWS + h * BLOCK, side * ROWS + (h + 1) * BLOCK)
            query = ref[:, h * HD : (h + 1) * HD]
            logits = jnp.where(allowed, dot(query, keys, NT), NEG)
            peak = jnp.max(logits, axis=1, keepdims=True)
            if side == 0:
                probs = jnp.exp2((logits - peak) * SCALE).astype(bf16)
                sums_ref[rows, :] = dot(probs, values)
            else:
                sums_ref[rows, :] = jnp.zeros((BLOCK, 2 * HD), f32)
            hi, mid, lo = split3(-peak)
            extra = jnp.where(col == 0, hi, jnp.where(col == 1, mid, jnp.where(col == 2, lo, 0.0)))
            extra = jnp.where(col == 3, 1.0, extra)
            wide_ref[rows, :] = jnp.concatenate([query, extra.astype(bf16)], 1)

    @pl.when((chip >= 5) | (core == 1))
    def _():
        blocks = [(rows_of(far_ref, 6), core == 1)]
        attend(wide_ref, sums_ref, blocks + [(rows_of(far_ref, i), chip >= d) for i, d in FAR_BLOCKS])


def rest_kernel(diagonal, place_ref, wide_ref, sums_in_ref, *refs):
    near_refs = refs[:4]
    kv_ref, far_ref, out_ref, sums_ref, peak_ref, held_ref = refs[4:]
    core, chip = place_ref[0] % 2, place_ref[0] // 2
    distances = near_blocks(core)
    sums_ref[...] = sums_in_ref[...]

    @pl.when(chip >= 1)
    def _():
        attend(
            wide_ref,
            sums_ref,
            [(rows_of(near_refs[i // 6], i % 6), chip >= d) for i, d in enumerate(distances)],
        )

    minus = jnp.where(iota((HD, HD), 0) < 3, -1.0, 0.0).astype(bf16)
    peak_ref[...] = dot(wide_ref[:, HD:], minus)

    @pl.when(jnp.logical_not(jnp.max(sums_ref[:, HD:]) < HUGE))
    def _():
        @pl.loop(0, LOCAL)
        def _(h):
            rows = pl.ds(pl.multiple_of(h * BLOCK, BLOCK), BLOCK)
            query = wide_ref[rows, :HD]
            whole = jnp.zeros((BLOCK, SHARE), jnp.int32)

            def add(carry, source, i, allowed):
                peak, total, summed = carry
                pltpu.sync_copy(source.at[pl.ds(pl.multiple_of(i * SHARE, SHARE), SHARE), :], held_ref)
                scores = jnp.where(allowed, dot(query, held_ref[:, :HD], NT), NEG)
                top = jnp.maximum(peak, jnp.max(scores, axis=1, keepdims=True))
                probs = jnp.where(allowed, jnp.exp2((scores - top) * SCALE), 0.0)
                factor = jnp.exp2((peak - top) * SCALE)
                total = factor * total + jnp.sum(probs, axis=1, keepdims=True)
                return top, total, factor * summed + dot(probs.astype(bf16), held_ref[:, HD:])

            def diagonal_part(j, carry):
                return add(carry, kv_ref, j, j * SHARE + iota((BLOCK, SHARE), 1) <= iota((BLOCK, SHARE), 0))

            def far_part(j, carry):
                distance = jnp.where(j < 6, 15 - j // 2 * 5, jnp.where(core == 1, 0, CHIPS))
                return add(carry, far_ref, j, whole + chip >= distance)

            carry = (jnp.full((BLOCK, 1), NEG, f32), jnp.zeros((BLOCK, 1), f32), jnp.zeros((BLOCK, HD), f32))
            if diagonal:
                carry = lax.fori_loop(0, 2, diagonal_part, carry)
            carry = lax.fori_loop(0, 7, far_part, carry)
            for source, ref in enumerate(near_refs):

                def near_part(j, carry):
                    return add(carry, ref, j, whole + chip >= distances[6 * source] - j // 2 * 5)

                carry = lax.fori_loop(0, 6, near_part, carry)
            peak, total, summed = carry
            sums_ref[rows, :] = jnp.concatenate([summed, jnp.broadcast_to(total, (BLOCK, HD))], 1)
            peak_ref[rows, :] = jnp.broadcast_to(peak, (BLOCK, HD))

    lane = iota((BLOCK, HD), 1)
    stats = jnp.zeros((BLOCK, HD), f32)
    for h in range(LOCAL):
        rows = slice(h * BLOCK, (h + 1) * BLOCK)
        out_ref[:, h * HD : (h + 1) * HD] = sums_ref[rows, :HD].astype(out_ref.dtype)
        stats = jnp.where(lane % LOCAL == h, jnp.where(lane < 3 * LOCAL, sums_ref[rows, HD:], peak_ref[rows, :]), stats)
    hi, mid, lo = split3(stats)
    part = lane // LOCAL % 3
    stats = jnp.where(part == 0, hi, jnp.where(part == 1, mid, lo))
    out_ref[:, LOCAL * HD :] = stats.astype(out_ref.dtype)


def merge_kernel(mine_ref, other_ref, out_ref):
    wide = LOCAL * HD
    lane, head = iota((HD, wide), 0), iota((HD, wide), 1) // HD

    def spread(ref, i):
        chosen = (lane // LOCAL // 3 == i) & (lane % LOCAL == head) & (lane < 6 * LOCAL)
        return dot(ref[:, wide:].astype(bf16), jnp.where(chosen, 1.0, 0.0).astype(bf16))

    here, there = spread(mine_ref, 1), spread(other_ref, 1)
    top = jnp.maximum(here, there)
    here, there = jnp.exp2((here - top) * SCALE), jnp.exp2((there - top) * SCALE)
    whole = here * spread(mine_ref, 0) + there * spread(other_ref, 0)
    summed = here * mine_ref[:, :wide].astype(f32) + there * other_ref[:, :wide].astype(f32)
    out_ref[...] = (summed / whole).astype(bf16)


def attention(place, query, kv, own, chip):
    core = place[0] % 2
    far = lax.ppermute(own, "seq", on_core(0, TEN) + on_core(1, FIVE))
    farther = lax.ppermute(own, "seq", on_core(0, FIFTEEN))
    near = bring(chip, (1, 2, 3))
    query, _ = after(query, chip)
    mate = lax.ppermute(query, "head", MATES)
    far = jnp.where(core == 0, jnp.concatenate([farther, far]), jnp.concatenate([far, own]))
    far = lax.all_gather(far, "seq", axis=0, tiled=True, axis_index_groups=PAIRS)
    out = lax.dynamic_slice_in_dim(far, (1 - core) * 2 * SHARE, 6 * SHARE, 0)
    next1 = lax.ppermute(out, "seq", on_core(0, UP1) + on_core(1, DOWN1))
    second1 = lax.ppermute(out, "seq", on_core(0, UP2) + on_core(1, DOWN2))
    _, *near = after(out, *near)
    near = join(*near)
    four = chained("window_state", [(0, 0)] + [(1, j) for j in JOINED], chip, near)
    four_far = bring(four, (4, 8, 12))
    far, _ = after(far, four)
    wide, sums = call(
        near_kernel,
        [shape(2 * ROWS, 2 * HD, dtype=bf16), shape(2 * ROWS, 2 * HD)],
        place,
        query,
        mate,
        kv,
        far,
        name="attend_near",
        limit=32,
        flops=4 * ROWS * 8 * BLOCK * 2 * HD,
    )
    next2 = lax.ppermute(next1, "seq", SWAP)
    second2 = lax.ppermute(second1, "seq", SWAP)
    wide, *four_far = after(wide, *four_far)

    def rest(side, dtype):
        def kernel(*refs):
            rest_kernel(side == 0, *refs)

        return pl.pallas_call(
            kernel,
            out_shape=shape(BLOCK, LOCAL * HD + HD, dtype=dtype),
            grid_spec=pltpu.PrefetchScalarGridSpec(
                num_scalar_prefetch=1,
                grid=(1,),
                in_specs=[pl.BlockSpec((ROWS, 2 * HD), lambda i, place: (side, 0))] * 2
                + [pl.BlockSpec(out.shape, lambda i, place: (0, 0))] * 4
                + [pl.BlockSpec(memory_space=pl.ANY)] * 2,
                out_specs=pl.BlockSpec((BLOCK, LOCAL * HD + HD), lambda i, place: (0, 0)),
                scratch_shapes=[
                    pltpu.VMEM((ROWS, 2 * HD), f32),
                    pltpu.VMEM((ROWS, HD), f32),
                    pltpu.VMEM((SHARE, 2 * HD), bf16),
                ],
            ),
            compiler_params=pltpu.CompilerParams(vmem_limit_bytes=32 * 2**20),
            cost_estimate=pl.CostEstimate(
                flops=4 * ROWS * 12 * BLOCK * 2 * HD, bytes_accessed=2**22, transcendentals=0
            ),
            name="attend_rest",
        )(place, wide, sums, next1, second1, next2, second2, kv, far)

    other = lax.ppermute(rest(1, bf16), "head", MATES)
    mine = rest(0, f32)
    soft_out = pl.pallas_call(merge_kernel, out_shape=shape(*query.shape, dtype=bf16), name="merge")(mine, other)
    return soft_out, near, four_far


def local(light_query, light_keys, light_values, log_decay, light_gain, query2, keys2, values2):
    place = jnp.stack([lax.axis_index("seq"), lax.axis_index("head")]).astype(jnp.int32)
    kv, share = pick(place, keys2, values2)
    own = lax.all_gather(share, "seq", axis=0, tiled=True, axis_index_groups=PAIRS)
    state_keys, _ = after(light_keys, own)
    both, chip = chip_states(state_keys, light_values, log_decay)
    soft_out, near, far = attention(place, query2, kv, own, chip)
    light_out = call(
        mix_kernel,
        shape(*light_query.shape, dtype=bf16),
        place,
        light_query,
        light_keys,
        light_values,
        log_decay,
        light_gain.reshape(1, LOCAL * HD),
        both,
        near,
        join(*far),
        name="mix",
    )
    return (light_out, soft_out)


def solution(mesh):
    placed = (
        P("seq", "head"),
        P("seq", "head"),
        P("seq", "head"),
        P("head", "seq"),
        P("head"),
        P("seq", "head"),
        P("seq", None),
        P("seq", None),
    )
    return jax.shard_map(
        local,
        mesh=mesh,
        in_specs=placed,
        out_specs=(P("seq", "head"), P("seq", "head")),
        check_vma=False,
    )
```

```python
import jax
import jax.numpy as jnp
from jax import lax
from jax.experimental import pallas as pl
from jax.experimental.pallas import tpu as pltpu
from jax.sharding import PartitionSpec as P

HEADS = 64
HD = 128
KVH = 8
BLOCK = 256
CHIPS = 16
LOCAL = 4
ROWS = LOCAL * BLOCK
SHARE = BLOCK // 2
SCALE = HD**-0.5 * 1.4426950408889634
NEG = -1e30
HUGE = 2.0**100
NT = (((1,), (1,)), ((), ()))
TN = (((0,), (0,)), ((), ()))
f32, bf16 = jnp.float32, jnp.bfloat16

def below(distance):
    return [(z, z + distance) for z in range(CHIPS - distance)]


FIVE = below(5) + [(11, 0), (12, 1)]
TEN = below(10) + [(6, 0), (7, 1)]
FIFTEEN = below(15) + [(1, 0), (2, 1)]
UP1 = [(z, z + 1) for z in range(15)]
UP2 = [(z, z + 2) for z in range(14)]
DOWN1 = [(z, z - 1) for z in range(5, 16)] + [(0, 15)]
DOWN2 = [(z, z - 2) for z in range(5, 16)] + [(0, 14), (1, 15)]


def on_core(core, chips):
    return [(2 * a + core, 2 * b + core) for a, b in chips]


PAIRS = [[s, s + 1] for s in range(0, 2 * CHIPS, 2)]
SWAP = [(s, s ^ 1) for s in range(2 * CHIPS)]
MATES = [(h, h ^ 1) for h in range(16)]


def iota(shape, dim):
    return lax.broadcasted_iota(jnp.int32, shape, dim)


def dot(a, b, dims=(((1,), (0,)), ((), ())), precision=None):
    return lax.dot_general(a, b, dims, precision=precision, preferred_element_type=f32)


def after(*values):
    return lax.optimization_barrier(values)


def split3(x):
    hi = x.astype(bf16).astype(f32)
    rest = x - hi
    mid = rest.astype(bf16).astype(f32)
    return hi, mid, rest - mid


def shape(*dims, dtype=f32):
    return jax.ShapeDtypeStruct(dims, dtype)


def call(kernel, out_shape, place, *args, left=0, scratch=(), name=None, flops=0, limit=16):
    def spec(dims):
        return pl.BlockSpec(dims, lambda i, place: (0,) * len(dims))

    many = isinstance(out_shape, list)
    outs = out_shape if many else [out_shape]
    specs = [spec(a.shape) for a in args]
    if left:
        specs[-left:] = [pl.BlockSpec(memory_space=pl.ANY)] * left
    out_specs = [spec(o.shape) for o in outs]
    return pl.pallas_call(
        kernel,
        out_shape=out_shape,
        grid_spec=pltpu.PrefetchScalarGridSpec(
            num_scalar_prefetch=1,
            grid=(1,),
            in_specs=specs,
            out_specs=out_specs if many else out_specs[0],
            scratch_shapes=scratch,
        ),
        compiler_params=pltpu.CompilerParams(vmem_limit_bytes=limit * 2**20),
        cost_estimate=pl.CostEstimate(
            flops=flops, bytes_accessed=sum(a.size * a.dtype.itemsize for a in args), transcendentals=0
        ),
        name=name,
    )(place, *args)


def pick_kernel(keys_ref, values_ref, out_ref, share_ref, sems):
    head = lax.axis_index("head")
    column = pl.ds(pl.multiple_of(head // 2 * HD, HD), HD)
    copies = [
        pltpu.make_async_copy(ref.at[:, column], out_ref.at[:, i * HD : (i + 1) * HD], sems.at[i])
        for i, ref in enumerate((keys_ref, values_ref))
    ]
    for copy in copies:
        copy.start()
    for copy in copies:
        copy.wait()
    start = pl.multiple_of(head % 2 * SHARE, SHARE)
    share_ref[...] = out_ref[pl.ds(start, SHARE), :]


def pick(keys2, values2):
    return pl.pallas_call(
        pick_kernel,
        out_shape=[shape(BLOCK, 2 * HD, dtype=bf16), shape(SHARE, 2 * HD, dtype=bf16)],
        in_specs=[pl.BlockSpec(memory_space=pl.ANY)] * 2,
        out_specs=[pl.BlockSpec(memory_space=pltpu.VMEM)] * 2,
        scratch_shapes=[pltpu.SemaphoreType.DMA((2,))],
        name="pick",
    )(keys2, values2)


STATE = LOCAL * HD
TAIL = 16
SENT = STATE + TAIL


def decay_columns(decay):
    lower = (iota((BLOCK, BLOCK), 1) <= iota((BLOCK, BLOCK), 0)).astype(f32)
    return dot(lower, decay, NT, lax.Precision.HIGHEST)


def told_rows(columns):
    lane, row = iota((TAIL, HD), 1), iota((TAIL, HD), 0)
    out = jnp.zeros((TAIL, HD), f32)
    for h, value in enumerate(columns):
        hi, mid, lo = split3(value)
        parts = jnp.where(row == 0, hi, jnp.where(row == 1, mid, jnp.where(row == 2, lo, 0.0)))
        out = jnp.where(lane == h, parts, out)
    return out.astype(bf16)


def told(rows):
    return jnp.sum(rows.astype(f32), axis=0, keepdims=True)


def state_kernel(keys_ref, values_ref, decay_ref, out_ref):
    running = decay_columns(decay_ref[...])
    last = running[BLOCK - 1 : BLOCK, :]
    tail = jnp.exp(last - running)
    for h in range(LOCAL):
        cols = slice(h * HD, (h + 1) * HD)
        scaled = (keys_ref[:, cols].astype(f32) * tail[:, h : h + 1]).astype(bf16)
        out_ref[cols, :] = dot(scaled, values_ref[:, cols], TN).astype(bf16)
    out_ref[STATE:, :] = told_rows([last[:, h : h + 1] for h in range(LOCAL)])


def chain(parts):
    decays = [told(part[STATE:, :]) for part in parts]

    def state(h):
        rows = slice(h * HD, (h + 1) * HD)
        out = parts[-1][rows, :].astype(f32)
        for part, decay in zip(parts[-2::-1], decays[-2::-1]):
            out = part[rows, :].astype(f32) + jnp.exp(decay[:, h : h + 1]) * out
        return out

    return state, sum(decays[1:], decays[0])


def chain_kernel(order, *refs):
    out_ref = refs[-1]
    state, total = chain([refs[i].at[j * SENT : (j + 1) * SENT] for i, j in order])
    for h in range(LOCAL):
        out_ref[h * HD : (h + 1) * HD, :] = state(h).astype(bf16)
    out_ref[STATE:, :] = told_rows([total[:, h : h + 1] for h in range(LOCAL)])


def chained(name, order, *arrays):
    def kernel(*refs):
        chain_kernel(order, *refs)

    return pl.pallas_call(kernel, out_shape=shape(SENT, HD, dtype=bf16), name=name)(*arrays)


JOINED = (0, 2, 1)


def join(first, second):
    return lax.all_gather(
        jnp.concatenate([first, second]), "seq", axis=0, tiled=True, axis_index_groups=PAIRS
    )


def last_kernel(
    place_ref,
    query_ref,
    keys_ref,
    values_ref,
    decay_ref,
    gain_ref,
    both_ref,
    near_ref,
    far_ref,
    mine_ref,
    other_ref,
    out_ref,
    soft_ref,
):
    add_sums(mine_ref, other_ref, soft_ref)
    core = place_ref[0] % 2
    decay = decay_ref[...]
    running = decay_columns(decay)
    upper = (iota((BLOCK, BLOCK), 0) <= iota((BLOCK, BLOCK), 1)).astype(f32)
    along = dot(decay, upper, precision=lax.Precision.HIGHEST)
    grow = jnp.exp(running)
    lower = iota((BLOCK, BLOCK), 1) <= iota((BLOCK, BLOCK), 0)
    first = jnp.exp(told(both_ref[STATE:SENT, :]))
    near, decays = chain([near_ref.at[j * SENT : (j + 1) * SENT] for j in JOINED])
    far, _ = chain([far_ref.at[j * SENT : (j + 1) * SENT] for j in JOINED])
    for h in range(LOCAL):
        cols = slice(h * HD, (h + 1) * HD)
        query = query_ref[:, cols]
        spread = jnp.where(lower, running[:, h : h + 1] - along[h : h + 1, :], NEG)
        weighted = (dot(query, keys_ref[:, cols], NT) * jnp.exp(spread)).astype(bf16)
        lifted = query.astype(f32) * grow[:, h : h + 1]
        high = lifted.astype(bf16)
        low = (lifted - high.astype(f32)).astype(bf16)
        state = near(h) + jnp.exp(decays[:, h : h + 1]) * far(h)
        after = first[:, h : h + 1] * state + both_ref[cols, :].astype(f32)
        state = jnp.where(core == 0, state, after).astype(bf16)
        mixed = dot(weighted, values_ref[:, cols]) + dot(high, state) + dot(low, state)
        norm = lax.rsqrt(jnp.mean(mixed * mixed, axis=-1, keepdims=True) + 1e-06)
        out_ref[:, cols] = (mixed * norm * gain_ref[:, cols]).astype(bf16)


def chip_states(keys, values, decay):
    mine = pl.pallas_call(state_kernel, out_shape=shape(SENT, HD, dtype=bf16), name="block_state")(
        keys, values, decay
    )
    both = lax.all_gather(mine, "seq", axis=0, tiled=True, axis_index_groups=PAIRS)
    return both, chained("chip_state", [(0, 1), (0, 0)], both)


def bring(state, distances):
    first, second, third = distances
    return (
        lax.ppermute(state, "seq", on_core(0, below(first)) + on_core(1, below(second))),
        lax.ppermute(state, "seq", on_core(0, below(third))),
    )


FAR_BLOCKS = tuple((i, 15 - 5 * (i // 2)) for i in range(6))


NEAR_BLOCKS = tuple(
    first - 5 * (i // 2) for hops in (2, 1) for first in (10 + hops, 15 - hops) for i in range(6)
)


def attend(wide_ref, sums_ref, blocks):
    col = iota((SHARE, HD), 1)
    counts = jnp.where(col < 3, 1.0, 0.0)
    misses = jnp.where(col < 3, 1.0, jnp.where(col == 3, NEG, 0.0))
    extra = jnp.concatenate([jnp.where(ok, counts, misses).astype(bf16) for _, ok in blocks], 0)
    kv = jnp.concatenate([rows for rows, _ in blocks], 0)
    keys = jnp.concatenate([kv[:, :HD], extra], 1)
    values = jnp.concatenate([kv[:, HD:], jnp.ones(extra.shape, bf16)], 1)
    tiles = sums_ref.shape[0] // BLOCK

    def logits(i):
        return dot(wide_ref[i * BLOCK : (i + 1) * BLOCK, :], keys, NT)

    ahead = logits(0)
    probs = None
    for i in range(tiles + 1):
        after = logits(i + 1) if i + 1 < tiles else None
        if probs is not None:
            sums_ref[(i - 1) * BLOCK : i * BLOCK, :] += dot(probs, values)
        if i < tiles:
            probs = jnp.exp2(ahead * SCALE).astype(bf16)
        ahead = after


def rows_of(ref, block):
    return ref[block * SHARE : (block + 1) * SHARE, :]


def near_kernel(place_ref, query_ref, mate_ref, kv_ref, far_ref, wide_ref, sums_ref):
    core, chip = place_ref[0] % 2, place_ref[0] // 2
    keys = kv_ref[:, :HD]
    values = jnp.concatenate([kv_ref[:, HD:], jnp.ones((BLOCK, HD), bf16)], 1)
    col = iota((BLOCK, HD), 1)
    allowed = iota((BLOCK, BLOCK), 1) <= iota((BLOCK, BLOCK), 0)
    for side, ref in enumerate((query_ref, mate_ref)):
        for h in range(LOCAL):
            rows = slice(side * ROWS + h * BLOCK, side * ROWS + (h + 1) * BLOCK)
            query = ref[:, h * HD : (h + 1) * HD]
            logits = jnp.where(allowed, dot(query, keys, NT), NEG)
            peak = jnp.max(logits, axis=1, keepdims=True)
            if side == 0:
                probs = jnp.exp2((logits - peak) * SCALE).astype(bf16)
                sums_ref[rows, :] = dot(probs, values)
            else:
                sums_ref[rows, :] = jnp.zeros((BLOCK, 2 * HD), f32)
            hi, mid, lo = split3(-peak)
            extra = jnp.where(col == 0, hi, jnp.where(col == 1, mid, jnp.where(col == 2, lo, 0.0)))
            extra = jnp.where(col == 3, 1.0, extra)
            wide_ref[rows, :] = jnp.concatenate([query, extra.astype(bf16)], 1)

    first = (rows_of(far_ref, 6), core == 1)

    @pl.when(chip >= 5)
    def _():
        attend(wide_ref, sums_ref, [first] + [(rows_of(far_ref, i), chip >= d) for i, d in FAR_BLOCKS])

    @pl.when((chip < 5) & (core == 1))
    def _():
        attend(wide_ref, sums_ref, [first])


def rest_kernel(mine, place_ref, wide_ref, sums_in_ref, *refs):
    near_refs = refs[:2]
    kv_ref, far_ref, out_ref, sums_ref, peak_ref, held_ref = refs[2:]
    core, chip = place_ref[0] % 2, place_ref[0] // 2
    sums_ref[...] = sums_in_ref[...]

    blocks = [(rows_of(near_refs[i // 12], i % 12), chip >= d, d) for i, d in enumerate(NEAR_BLOCKS)]

    @pl.when(chip >= 5)
    def _():
        attend(wide_ref, sums_ref, [(rows, ok) for rows, ok, _ in blocks])

    @pl.when((chip >= 1) & (chip < 5))
    def _():
        attend(wide_ref, sums_ref, [(rows, ok) for rows, ok, d in blocks if d < 5])

    minus = jnp.where(iota((HD, HD), 0) < 3, -1.0, 0.0).astype(bf16)
    peak_ref[...] = dot(wide_ref[:, HD:], minus)

    @pl.when(jnp.logical_not(jnp.max(sums_ref[:, HD:]) < HUGE))
    def _():
        @pl.loop(0, LOCAL)
        def _(h):
            rows = pl.ds(pl.multiple_of(h * BLOCK, BLOCK), BLOCK)
            query = wide_ref[rows, :HD]
            whole = jnp.zeros((BLOCK, SHARE), jnp.int32)

            def add(carry, source, i, allowed):
                peak, total, summed = carry
                pltpu.sync_copy(source.at[pl.ds(pl.multiple_of(i * SHARE, SHARE), SHARE), :], held_ref)
                scores = jnp.where(allowed, dot(query, held_ref[:, :HD], NT), NEG)
                top = jnp.maximum(peak, jnp.max(scores, axis=1, keepdims=True))
                probs = jnp.where(allowed, jnp.exp2((scores - top) * SCALE), 0.0)
                factor = jnp.exp2((peak - top) * SCALE)
                total = factor * total + jnp.sum(probs, axis=1, keepdims=True)
                return top, total, factor * summed + dot(probs.astype(bf16), held_ref[:, HD:])

            def diagonal_part(j, carry):
                return add(carry, kv_ref, j, j * SHARE + iota((BLOCK, SHARE), 1) <= iota((BLOCK, SHARE), 0))

            def far_part(j, carry):
                distance = jnp.where(j < 6, 15 - j // 2 * 5, jnp.where(core == 1, 0, CHIPS))
                return add(carry, far_ref, j, whole + chip >= distance)

            carry = (jnp.full((BLOCK, 1), NEG, f32), jnp.zeros((BLOCK, 1), f32), jnp.zeros((BLOCK, HD), f32))
            if mine:
                carry = lax.fori_loop(0, 2, diagonal_part, carry)
            carry = lax.fori_loop(0, 7, far_part, carry)
            for source, ref in enumerate(near_refs):

                def near_part(j, carry):
                    first = jnp.where(j < 6, 12 - source, 13 + source)
                    return add(carry, ref, j, whole + chip >= first - j % 6 // 2 * 5)

                carry = lax.fori_loop(0, 12, near_part, carry)
            peak, total, summed = carry
            sums_ref[rows, :] = jnp.concatenate([summed, jnp.broadcast_to(total, (BLOCK, HD))], 1)
            peak_ref[rows, :] = jnp.broadcast_to(peak, (BLOCK, HD))

    lane = iota((BLOCK, HD), 1)
    stats = jnp.zeros((BLOCK, HD), f32)
    for h in range(LOCAL):
        rows = slice(h * BLOCK, (h + 1) * BLOCK)
        out_ref[:, h * HD : (h + 1) * HD] = sums_ref[rows, :HD].astype(out_ref.dtype)
        stats = jnp.where(lane % LOCAL == h, jnp.where(lane < 3 * LOCAL, sums_ref[rows, HD:], peak_ref[rows, :]), stats)
    hi, mid, lo = split3(stats)
    part = lane // LOCAL % 3
    stats = jnp.where(part == 0, hi, jnp.where(part == 1, mid, lo))
    out_ref[:, LOCAL * HD :] = stats.astype(out_ref.dtype)


def add_sums(mine_ref, other_ref, out_ref):
    wide = LOCAL * HD
    lane, head = iota((HD, wide), 0), iota((HD, wide), 1) // HD

    def spread(ref, i):
        chosen = (lane // LOCAL // 3 == i) & (lane % LOCAL == head) & (lane < 6 * LOCAL)
        return dot(ref[:, wide:].astype(bf16), jnp.where(chosen, 1.0, 0.0).astype(bf16))

    here, there = spread(mine_ref, 1), spread(other_ref, 1)
    top = jnp.maximum(here, there)
    here, there = jnp.exp2((here - top) * SCALE), jnp.exp2((there - top) * SCALE)
    whole = here * spread(mine_ref, 0) + there * spread(other_ref, 0)
    summed = here * mine_ref[:, :wide] + there * other_ref[:, :wide].astype(f32)
    out_ref[...] = (summed / whole).astype(bf16)


def attention(place, query, kv, own, chip):
    core = place[0] % 2
    far = lax.ppermute(own, "seq", on_core(0, TEN) + on_core(1, FIVE))
    farther = lax.ppermute(own, "seq", on_core(0, FIFTEEN))
    query, farther = after(query, farther)
    near = bring(chip, (1, 2, 3))
    query, _ = after(query, chip)
    mate = lax.ppermute(query, "head", MATES)
    far = jnp.where(core == 0, jnp.concatenate([farther, far]), jnp.concatenate([far, own]))
    far = lax.all_gather(far, "seq", axis=0, tiled=True, axis_index_groups=PAIRS)
    out = lax.dynamic_slice_in_dim(far, (1 - core) * 2 * SHARE, 6 * SHARE, 0)
    next1 = lax.ppermute(out, "seq", on_core(0, UP1) + on_core(1, DOWN1))
    second1 = lax.ppermute(out, "seq", on_core(0, UP2) + on_core(1, DOWN2))
    _, *near = after(out, *near)
    near = join(*near)
    four = chained("window_state", [(0, 0)] + [(1, j) for j in JOINED], chip, near)
    four_far = bring(four, (4, 8, 12))
    far, _ = after(far, four)
    wide, sums = call(
        near_kernel,
        [shape(2 * ROWS, 2 * HD, dtype=bf16), shape(2 * ROWS, 2 * HD)],
        place,
        query,
        mate,
        kv,
        far,
        name="attend_near",
        limit=32,
        flops=4 * ROWS * 8 * BLOCK * 2 * HD,
    )
    next1 = lax.all_gather(next1, "seq", axis=0, tiled=True, axis_index_groups=PAIRS)
    second1 = lax.all_gather(second1, "seq", axis=0, tiled=True, axis_index_groups=PAIRS)

    def rest(side, dtype):
        def kernel(*refs):
            rest_kernel(side == 0, *refs)

        out = shape(BLOCK, LOCAL * HD + HD, dtype=dtype)
        return pl.pallas_call(
            kernel,
            out_shape=out,
            grid_spec=pltpu.PrefetchScalarGridSpec(
                num_scalar_prefetch=1,
                grid=(1,),
                in_specs=[pl.BlockSpec((ROWS, 2 * HD), lambda i, place: (side, 0))] * 2
                + [pl.BlockSpec(next1.shape, lambda i, place: (0, 0))] * 2
                + [pl.BlockSpec(memory_space=pl.ANY)] * 2,
                out_specs=pl.BlockSpec(out.shape, lambda i, place: (0, 0)),
                scratch_shapes=[
                    pltpu.VMEM((ROWS, 2 * HD), f32),
                    pltpu.VMEM((ROWS, HD), f32),
                    pltpu.VMEM((SHARE, 2 * HD), bf16),
                ],
            ),
            compiler_params=pltpu.CompilerParams(vmem_limit_bytes=32 * 2**20),
            cost_estimate=pl.CostEstimate(flops=0, bytes_accessed=0, transcendentals=0),
            name="attend_rest",
        )(place, wide, sums, second1, next1, kv, far)

    send = rest(1, bf16)
    other = lax.ppermute(send, "head", MATES)
    wide, *four_far = after(wide, *four_far, send)[:-1]
    return rest(0, f32), other, near, four_far


def local(light_query, light_keys, light_values, log_decay, light_gain, query2, keys2, values2):
    place = jnp.stack([lax.axis_index("seq"), lax.axis_index("head")]).astype(jnp.int32)
    kv, share = pick(keys2, values2)
    own = lax.all_gather(share, "seq", axis=0, tiled=True, axis_index_groups=PAIRS)
    state_keys, _ = after(light_keys, own)
    both, chip = chip_states(state_keys, light_values, log_decay)
    mine, other, near, far = attention(place, query2, kv, own, chip)
    out = shape(*light_query.shape, dtype=bf16)
    light_out, soft_out = call(
        last_kernel,
        [out, out],
        place,
        light_query,
        light_keys,
        light_values,
        log_decay,
        light_gain.reshape(1, LOCAL * HD),
        both,
        near,
        join(*far),
        mine,
        other,
        name="mix_and_add",
    )
    return (light_out, soft_out)


def solution(mesh):
    placed = (
        P("seq", "head"),
        P("seq", "head"),
        P("seq", "head"),
        P("head", "seq"),
        P("head"),
        P("seq", "head"),
        P("seq", None),
        P("seq", None),
    )
    return jax.shard_map(
        local,
        mesh=mesh,
        in_specs=placed,
        out_specs=(P("seq", "head"), P("seq", "head")),
        check_vma=False,
    )
```

```python
import jax
import jax.numpy as jnp
from jax import lax
from jax.experimental import pallas as pl
from jax.experimental.pallas import tpu as pltpu
from jax.sharding import PartitionSpec as P

HEADS = 64
HD = 128
KVH = 8
BLOCK = 256
CHIPS = 16
LOCAL = 4
ROWS = LOCAL * BLOCK
SHARE = BLOCK // 2
SCALE = HD**-0.5 * 1.4426950408889634
NEG = -1e30
HUGE = 2.0**100
NT = (((1,), (1,)), ((), ()))
TN = (((0,), (0,)), ((), ()))
f32, bf16 = jnp.float32, jnp.bfloat16

def below(distance):
    return [(z, z + distance) for z in range(CHIPS - distance)]


FIVE = below(5) + [(11, 0), (12, 1)]
TEN = below(10) + [(6, 0), (7, 1)]
FIFTEEN = below(15) + [(1, 0), (2, 1)]
UP1 = [(z, z + 1) for z in range(15)]
UP2 = [(z, z + 2) for z in range(14)]
DOWN1 = [(z, z - 1) for z in range(5, 16)] + [(0, 15)]
DOWN2 = [(z, z - 2) for z in range(5, 16)] + [(0, 14), (1, 15)]


def on_core(core, chips):
    return [(2 * a + core, 2 * b + core) for a, b in chips]


PAIRS = [[s, s + 1] for s in range(0, 2 * CHIPS, 2)]
SWAP = [(s, s ^ 1) for s in range(2 * CHIPS)]
MATES = [(h, h ^ 1) for h in range(16)]


def iota(shape, dim):
    return lax.broadcasted_iota(jnp.int32, shape, dim)


def dot(a, b, dims=(((1,), (0,)), ((), ())), precision=None):
    return lax.dot_general(a, b, dims, precision=precision, preferred_element_type=f32)


def after(*values):
    return lax.optimization_barrier(values)


def split3(x):
    hi = x.astype(bf16).astype(f32)
    rest = x - hi
    mid = rest.astype(bf16).astype(f32)
    return hi, mid, rest - mid


def shape(*dims, dtype=f32):
    return jax.ShapeDtypeStruct(dims, dtype)


def call(kernel, out_shape, place, *args, left=0, scratch=(), name=None, flops=0, limit=16):
    def spec(dims):
        return pl.BlockSpec(dims, lambda i, place: (0,) * len(dims))

    many = isinstance(out_shape, list)
    outs = out_shape if many else [out_shape]
    specs = [spec(a.shape) for a in args]
    if left:
        specs[-left:] = [pl.BlockSpec(memory_space=pl.ANY)] * left
    out_specs = [spec(o.shape) for o in outs]
    return pl.pallas_call(
        kernel,
        out_shape=out_shape,
        grid_spec=pltpu.PrefetchScalarGridSpec(
            num_scalar_prefetch=1,
            grid=(1,),
            in_specs=specs,
            out_specs=out_specs if many else out_specs[0],
            scratch_shapes=scratch,
        ),
        compiler_params=pltpu.CompilerParams(vmem_limit_bytes=limit * 2**20),
        cost_estimate=pl.CostEstimate(
            flops=flops, bytes_accessed=sum(a.size * a.dtype.itemsize for a in args), transcendentals=0
        ),
        name=name,
    )(place, *args)


def pick_kernel(keys_ref, values_ref, out_ref, share_ref, sems):
    head = lax.axis_index("head")
    column = pl.ds(pl.multiple_of(head // 2 * HD, HD), HD)
    copies = [
        pltpu.make_async_copy(ref.at[:, column], out_ref.at[:, i * HD : (i + 1) * HD], sems.at[i])
        for i, ref in enumerate((keys_ref, values_ref))
    ]
    for copy in copies:
        copy.start()
    for copy in copies:
        copy.wait()
    start = pl.multiple_of(head % 2 * SHARE, SHARE)
    share_ref[...] = out_ref[pl.ds(start, SHARE), :]


def pick(keys2, values2):
    return pl.pallas_call(
        pick_kernel,
        out_shape=[shape(BLOCK, 2 * HD, dtype=bf16), shape(SHARE, 2 * HD, dtype=bf16)],
        in_specs=[pl.BlockSpec(memory_space=pl.ANY)] * 2,
        out_specs=[pl.BlockSpec(memory_space=pltpu.VMEM)] * 2,
        scratch_shapes=[pltpu.SemaphoreType.DMA((2,))],
        name="pick",
    )(keys2, values2)


STATE = LOCAL * HD
TAIL = 16
SENT = STATE + TAIL


def decay_columns(decay):
    lower = (iota((BLOCK, BLOCK), 1) <= iota((BLOCK, BLOCK), 0)).astype(f32)
    return dot(lower, decay, NT, lax.Precision.HIGHEST)


def told_rows(columns):
    lane, row = iota((TAIL, HD), 1), iota((TAIL, HD), 0)
    out = jnp.zeros((TAIL, HD), f32)
    for h, value in enumerate(columns):
        hi, mid, lo = split3(value)
        parts = jnp.where(row == 0, hi, jnp.where(row == 1, mid, jnp.where(row == 2, lo, 0.0)))
        out = jnp.where(lane == h, parts, out)
    return out.astype(bf16)


def told(rows):
    return jnp.sum(rows.astype(f32), axis=0, keepdims=True)


def state_kernel(keys_ref, values_ref, decay_ref, out_ref):
    running = decay_columns(decay_ref[...])
    last = running[BLOCK - 1 : BLOCK, :]
    tail = jnp.exp(last - running)
    for h in range(LOCAL):
        cols = slice(h * HD, (h + 1) * HD)
        scaled = (keys_ref[:, cols].astype(f32) * tail[:, h : h + 1]).astype(bf16)
        out_ref[cols, :] = dot(scaled, values_ref[:, cols], TN).astype(bf16)
    out_ref[STATE:, :] = told_rows([last[:, h : h + 1] for h in range(LOCAL)])


def chain(parts):
    decays = [told(part[STATE:, :]) for part in parts]

    def state(h):
        rows = slice(h * HD, (h + 1) * HD)
        out = parts[-1][rows, :].astype(f32)
        for part, decay in zip(parts[-2::-1], decays[-2::-1]):
            out = part[rows, :].astype(f32) + jnp.exp(decay[:, h : h + 1]) * out
        return out

    return state, sum(decays[1:], decays[0])


def chain_kernel(order, *refs):
    out_ref = refs[-1]
    state, total = chain([refs[i].at[j * SENT : (j + 1) * SENT] for i, j in order])
    for h in range(LOCAL):
        out_ref[h * HD : (h + 1) * HD, :] = state(h).astype(bf16)
    out_ref[STATE:, :] = told_rows([total[:, h : h + 1] for h in range(LOCAL)])


def chained(name, order, *arrays):
    def kernel(*refs):
        chain_kernel(order, *refs)

    return pl.pallas_call(kernel, out_shape=shape(SENT, HD, dtype=bf16), name=name)(*arrays)


JOINED = (0, 2, 1)


def join(first, second):
    return lax.all_gather(
        jnp.concatenate([first, second]), "seq", axis=0, tiled=True, axis_index_groups=PAIRS
    )


def last_kernel(
    place_ref,
    query_ref,
    keys_ref,
    values_ref,
    decay_ref,
    gain_ref,
    both_ref,
    near_ref,
    far_ref,
    out_ref,
):
    core = place_ref[0] % 2
    decay = decay_ref[...]
    running = decay_columns(decay)
    upper = (iota((BLOCK, BLOCK), 0) <= iota((BLOCK, BLOCK), 1)).astype(f32)
    along = dot(decay, upper, precision=lax.Precision.HIGHEST)
    grow = jnp.exp(running)
    lower = iota((BLOCK, BLOCK), 1) <= iota((BLOCK, BLOCK), 0)
    first = jnp.exp(told(both_ref[STATE:SENT, :]))
    near, decays = chain([near_ref.at[j * SENT : (j + 1) * SENT] for j in JOINED])
    far, _ = chain([far_ref.at[j * SENT : (j + 1) * SENT] for j in JOINED])
    for h in range(LOCAL):
        cols = slice(h * HD, (h + 1) * HD)
        query = query_ref[:, cols]
        spread = jnp.where(lower, running[:, h : h + 1] - along[h : h + 1, :], NEG)
        weighted = (dot(query, keys_ref[:, cols], NT) * jnp.exp(spread)).astype(bf16)
        lifted = query.astype(f32) * grow[:, h : h + 1]
        high = lifted.astype(bf16)
        low = (lifted - high.astype(f32)).astype(bf16)
        state = near(h) + jnp.exp(decays[:, h : h + 1]) * far(h)
        after = first[:, h : h + 1] * state + both_ref[cols, :].astype(f32)
        state = jnp.where(core == 0, state, after).astype(bf16)
        mixed = dot(weighted, values_ref[:, cols]) + dot(high, state) + dot(low, state)
        norm = lax.rsqrt(jnp.mean(mixed * mixed, axis=-1, keepdims=True) + 1e-06)
        out_ref[:, cols] = (mixed * norm * gain_ref[:, cols]).astype(bf16)


def chip_states(keys, values, decay):
    mine = pl.pallas_call(state_kernel, out_shape=shape(SENT, HD, dtype=bf16), name="block_state")(
        keys, values, decay
    )
    both = lax.all_gather(mine, "seq", axis=0, tiled=True, axis_index_groups=PAIRS)
    return both, chained("chip_state", [(0, 1), (0, 0)], both)


def bring(state, distances):
    first, second, third = distances
    return (
        lax.ppermute(state, "seq", on_core(0, below(first)) + on_core(1, below(second))),
        lax.ppermute(state, "seq", on_core(0, below(third))),
    )


FAR_BLOCKS = tuple((i, 15 - 5 * (i // 2)) for i in range(6))


NEAR_BLOCKS = tuple(
    first - 5 * (i // 2) for hops in (2, 1) for first in (10 + hops, 15 - hops) for i in range(6)
)


def attend(wide_ref, sums_ref, blocks):
    col = iota((SHARE, HD), 1)
    counts = jnp.where(col < 3, 1.0, 0.0)
    misses = jnp.where(col < 3, 1.0, jnp.where(col == 3, NEG, 0.0))
    extra = jnp.concatenate([jnp.where(ok, counts, misses).astype(bf16) for _, ok in blocks], 0)
    kv = jnp.concatenate([rows for rows, _ in blocks], 0)
    keys = jnp.concatenate([kv[:, :HD], extra], 1)
    values = jnp.concatenate([kv[:, HD:], jnp.ones(extra.shape, bf16)], 1)
    tiles = sums_ref.shape[0] // BLOCK

    def logits(i):
        return dot(wide_ref[i * BLOCK : (i + 1) * BLOCK, :], keys, NT)

    ahead = logits(0)
    probs = None
    for i in range(tiles + 1):
        after = logits(i + 1) if i + 1 < tiles else None
        if probs is not None:
            sums_ref[(i - 1) * BLOCK : i * BLOCK, :] += dot(probs, values)
        if i < tiles:
            probs = jnp.exp2(ahead * SCALE).astype(bf16)
        ahead = after


def rows_of(ref, block):
    return ref[block * SHARE : (block + 1) * SHARE, :]


def near_kernel(place_ref, query_ref, mate_ref, kv_ref, far_ref, wide_ref, sums_ref):
    core, chip = place_ref[0] % 2, place_ref[0] // 2
    keys = kv_ref[:, :HD]
    values = jnp.concatenate([kv_ref[:, HD:], jnp.ones((BLOCK, HD), bf16)], 1)
    col = iota((BLOCK, HD), 1)
    allowed = iota((BLOCK, BLOCK), 1) <= iota((BLOCK, BLOCK), 0)
    for side, ref in enumerate((query_ref, mate_ref)):
        for h in range(LOCAL):
            rows = slice(side * ROWS + h * BLOCK, side * ROWS + (h + 1) * BLOCK)
            query = ref[:, h * HD : (h + 1) * HD]
            logits = jnp.where(allowed, dot(query, keys, NT), NEG)
            peak = jnp.max(logits, axis=1, keepdims=True)
            if side == 0:
                probs = jnp.exp2((logits - peak) * SCALE).astype(bf16)
                sums_ref[rows, :] = dot(probs, values)
            else:
                sums_ref[rows, :] = jnp.zeros((BLOCK, 2 * HD), f32)
            hi, mid, lo = split3(-peak)
            extra = jnp.where(col == 0, hi, jnp.where(col == 1, mid, jnp.where(col == 2, lo, 0.0)))
            extra = jnp.where(col == 3, 1.0, extra)
            wide_ref[rows, :] = jnp.concatenate([query, extra.astype(bf16)], 1)

    first = (rows_of(far_ref, 6), core == 1)

    @pl.when(chip >= 5)
    def _():
        attend(wide_ref, sums_ref, [first] + [(rows_of(far_ref, i), chip >= d) for i, d in FAR_BLOCKS])

    @pl.when((chip < 5) & (core == 1))
    def _():
        attend(wide_ref, sums_ref, [first])


def rest_kernel(mine, place_ref, wide_ref, sums_in_ref, *refs):
    near_refs = refs[:2]
    kv_ref, far_ref, out_ref, sums_ref, peak_ref, held_ref = refs[2:]
    core, chip = place_ref[0] % 2, place_ref[0] // 2
    sums_ref[...] = sums_in_ref[...]

    blocks = [(rows_of(near_refs[i // 12], i % 12), chip >= d, d) for i, d in enumerate(NEAR_BLOCKS)]

    @pl.when(chip >= 5)
    def _():
        attend(wide_ref, sums_ref, [(rows, ok) for rows, ok, _ in blocks])

    @pl.when((chip >= 1) & (chip < 5))
    def _():
        attend(wide_ref, sums_ref, [(rows, ok) for rows, ok, d in blocks if d < 5])

    minus = jnp.where(iota((HD, HD), 0) < 3, -1.0, 0.0).astype(bf16)
    peak_ref[...] = dot(wide_ref[:, HD:], minus)

    @pl.when(jnp.logical_not(jnp.max(sums_ref[:, HD:]) < HUGE))
    def _():
        @pl.loop(0, LOCAL)
        def _(h):
            rows = pl.ds(pl.multiple_of(h * BLOCK, BLOCK), BLOCK)
            query = wide_ref[rows, :HD]
            whole = jnp.zeros((BLOCK, SHARE), jnp.int32)

            def add(carry, source, i, allowed):
                peak, total, summed = carry
                pltpu.sync_copy(source.at[pl.ds(pl.multiple_of(i * SHARE, SHARE), SHARE), :], held_ref)
                scores = jnp.where(allowed, dot(query, held_ref[:, :HD], NT), NEG)
                top = jnp.maximum(peak, jnp.max(scores, axis=1, keepdims=True))
                probs = jnp.where(allowed, jnp.exp2((scores - top) * SCALE), 0.0)
                factor = jnp.exp2((peak - top) * SCALE)
                total = factor * total + jnp.sum(probs, axis=1, keepdims=True)
                return top, total, factor * summed + dot(probs.astype(bf16), held_ref[:, HD:])

            def diagonal_part(j, carry):
                return add(carry, kv_ref, j, j * SHARE + iota((BLOCK, SHARE), 1) <= iota((BLOCK, SHARE), 0))

            def far_part(j, carry):
                distance = jnp.where(j < 6, 15 - j // 2 * 5, jnp.where(core == 1, 0, CHIPS))
                return add(carry, far_ref, j, whole + chip >= distance)

            carry = (jnp.full((BLOCK, 1), NEG, f32), jnp.zeros((BLOCK, 1), f32), jnp.zeros((BLOCK, HD), f32))
            if mine:
                carry = lax.fori_loop(0, 2, diagonal_part, carry)
            carry = lax.fori_loop(0, 7, far_part, carry)
            for source, ref in enumerate(near_refs):

                def near_part(j, carry):
                    first = jnp.where(j < 6, 12 - source, 13 + source)
                    return add(carry, ref, j, whole + chip >= first - j % 6 // 2 * 5)

                carry = lax.fori_loop(0, 12, near_part, carry)
            peak, total, summed = carry
            sums_ref[rows, :] = jnp.concatenate([summed, jnp.broadcast_to(total, (BLOCK, HD))], 1)
            peak_ref[rows, :] = jnp.broadcast_to(peak, (BLOCK, HD))

    lane = iota((BLOCK, HD), 1)
    stats = jnp.zeros((BLOCK, HD), f32)
    for h in range(LOCAL):
        rows = slice(h * BLOCK, (h + 1) * BLOCK)
        out_ref[:, h * HD : (h + 1) * HD] = sums_ref[rows, :HD].astype(out_ref.dtype)
        stats = jnp.where(lane % LOCAL == h, jnp.where(lane < 3 * LOCAL, sums_ref[rows, HD:], peak_ref[rows, :]), stats)
    hi, mid, lo = split3(stats)
    part = lane // LOCAL % 3
    stats = jnp.where(part == 0, hi, jnp.where(part == 1, mid, lo))
    out_ref[:, LOCAL * HD :] = stats.astype(out_ref.dtype)


def add_sums(mine_ref, other_ref, out_ref):
    wide = LOCAL * HD
    lane, head = iota((HD, wide), 0), iota((HD, wide), 1) // HD

    def spread(ref, i):
        chosen = (lane // LOCAL // 3 == i) & (lane % LOCAL == head) & (lane < 6 * LOCAL)
        return dot(ref[:, wide:].astype(bf16), jnp.where(chosen, 1.0, 0.0).astype(bf16))

    here, there = spread(mine_ref, 1), spread(other_ref, 1)
    top = jnp.maximum(here, there)
    here, there = jnp.exp2((here - top) * SCALE), jnp.exp2((there - top) * SCALE)
    whole = here * spread(mine_ref, 0) + there * spread(other_ref, 0)
    summed = here * mine_ref[:, :wide] + there * other_ref[:, :wide].astype(f32)
    out_ref[...] = (summed / whole).astype(bf16)


def attention(place, query, kv, own, chip):
    core = place[0] % 2
    far = lax.ppermute(own, "seq", on_core(0, TEN) + on_core(1, FIVE))
    farther = lax.ppermute(own, "seq", on_core(0, FIFTEEN))
    query, farther = after(query, farther)
    near = bring(chip, (1, 2, 3))
    query, _ = after(query, chip)
    mate = lax.ppermute(query, "head", MATES)
    far = jnp.where(core == 0, jnp.concatenate([farther, far]), jnp.concatenate([far, own]))
    far = lax.all_gather(far, "seq", axis=0, tiled=True, axis_index_groups=PAIRS)
    out = lax.dynamic_slice_in_dim(far, (1 - core) * 2 * SHARE, 6 * SHARE, 0)
    next1 = lax.ppermute(out, "seq", on_core(0, UP1) + on_core(1, DOWN1))
    second1 = lax.ppermute(out, "seq", on_core(0, UP2) + on_core(1, DOWN2))
    _, *near = after(out, *near)
    near = join(*near)
    four = chained("window_state", [(0, 0)] + [(1, j) for j in JOINED], chip, near)
    four_far = bring(four, (4, 8, 12))
    far, _ = after(far, four)
    wide, sums = call(
        near_kernel,
        [shape(2 * ROWS, 2 * HD, dtype=bf16), shape(2 * ROWS, 2 * HD)],
        place,
        query,
        mate,
        kv,
        far,
        name="attend_near",
        limit=32,
        flops=4 * ROWS * 8 * BLOCK * 2 * HD,
    )
    next1 = lax.all_gather(next1, "seq", axis=0, tiled=True, axis_index_groups=PAIRS)
    second1 = lax.all_gather(second1, "seq", axis=0, tiled=True, axis_index_groups=PAIRS)

    def rest(side, dtype):
        def kernel(*refs):
            rest_kernel(side == 0, *refs)

        out = shape(BLOCK, LOCAL * HD + HD, dtype=dtype)
        return pl.pallas_call(
            kernel,
            out_shape=out,
            grid_spec=pltpu.PrefetchScalarGridSpec(
                num_scalar_prefetch=1,
                grid=(1,),
                in_specs=[pl.BlockSpec((ROWS, 2 * HD), lambda i, place: (side, 0))] * 2
                + [pl.BlockSpec(next1.shape, lambda i, place: (0, 0))] * 2
                + [pl.BlockSpec(memory_space=pl.ANY)] * 2,
                out_specs=pl.BlockSpec(out.shape, lambda i, place: (0, 0)),
                scratch_shapes=[
                    pltpu.VMEM((ROWS, 2 * HD), f32),
                    pltpu.VMEM((ROWS, HD), f32),
                    pltpu.VMEM((SHARE, 2 * HD), bf16),
                ],
            ),
            compiler_params=pltpu.CompilerParams(vmem_limit_bytes=32 * 2**20),
            cost_estimate=pl.CostEstimate(flops=0, bytes_accessed=0, transcendentals=0),
            name="attend_rest",
        )(place, wide, sums, second1, next1, kv, far)

    send = rest(1, bf16)
    other = lax.ppermute(send, "head", MATES)
    wide, *four_far = after(wide, *four_far, send)[:-1]
    return rest(0, f32), other, near, four_far


def local(light_query, light_keys, light_values, log_decay, light_gain, query2, keys2, values2):
    place = jnp.stack([lax.axis_index("seq"), lax.axis_index("head")]).astype(jnp.int32)
    kv, share = pick(keys2, values2)
    own = lax.all_gather(share, "seq", axis=0, tiled=True, axis_index_groups=PAIRS)
    state_keys, _ = after(light_keys, own)
    both, chip = chip_states(state_keys, light_values, log_decay)
    mine, other, near, far = attention(place, query2, kv, own, chip)
    out = shape(*light_query.shape, dtype=bf16)
    light_out = call(
        last_kernel,
        out,
        place,
        light_query,
        light_keys,
        light_values,
        log_decay,
        light_gain.reshape(1, LOCAL * HD),
        both,
        near,
        join(*far),
        name="mix",
    )
    other, _ = after(other, light_out)
    soft_out = pl.pallas_call(add_sums, out_shape=out, name="add_sums")(mine, other)
    return (light_out, soft_out)


def solution(mesh):
    placed = (
        P("seq", "head"),
        P("seq", "head"),
        P("seq", "head"),
        P("head", "seq"),
        P("head"),
        P("seq", "head"),
        P("seq", None),
        P("seq", None),
    )
    return jax.shard_map(
        local,
        mesh=mesh,
        in_specs=placed,
        out_specs=(P("seq", "head"), P("seq", "head")),
        check_vma=False,
    )
```
